32 devices in a mesh: blk: 16 (over z, y, x), head: 2 (over core).
Axes of the slice: x: 2, y: 2, z: 4, core: 2. Of those that a mesh axis runs over, the one named last changes fastest.
Arguments:
- vision: bfloat16 [16, 1601, 8192], P('blk', None, 'head'), may hold values from -6 to 6
- kept_index: int32 [16, 128], P('blk'), may hold values from 0 to 1600, as said below
- w_key: bfloat16 [8192, 1024], P('head', 'blk'), may hold values from -0.0625 to 0.0625
- w_value: bfloat16 [8192, 1024], P('head', 'blk'), may hold values from -0.0625 to 0.0625
- queries: bfloat16 [2048, 8192], P('blk', 'head'), may hold values from -140 to 140
- last_frame: int32 [2048], P('blk'), may hold values from 0 to 15, as said below
- attn_gate: float32 [1], replicated, may hold values from 0.3 to 1.5
Outputs:
- gated: bfloat16 [2048, 8192], P('blk', 'head')
The draws below stay inside these ranges and needn't reach their ends.
Inputs may be any that keep to these rules, and one draw needn't show every extreme that they name: `kept_index`: each frame's indices are distinct; index 0 (the class token) and index 1600 are kept in every frame. `last_frame`: never falls from one row to the next; row 0 sees only frame 0, the last row sees all frames, and every frame is the last frame of at least one row.
All inputs are finite; a program needn't handle non-finite values.
Results may differ from the reference program's by a relative error of at most 0.012.
The reference program's roundings to bfloat16 on the way count: a program that leaves them out, or rounds other values in their place, can miss the bound.
Values may be sent and summed in bfloat16 or wider, within the bound.
A program may use at most 128 MiB of HBM per device.

```python
import jax
import jax.numpy as jnp
from jax import lax

D = 8192
HEADS = 64
KV_HEADS = 8
HD = 128
PATCHES = 1601
KEPT = 128
TEXT = 2048
FRAMES = 16


def draw_kept_index(key, part):
    key = jax.random.fold_in(key, 5)
    frame_keys = jax.random.split(key, FRAMES)

    def choose_frame(frame_key):
        shuffled = jax.random.permutation(frame_key, PATCHES - 2) + 1
        return jnp.sort(shuffled[:KEPT - 2])
    inner = jax.vmap(choose_frame)(frame_keys).astype(jnp.int32)
    first = jnp.zeros((FRAMES, 1), jnp.int32)
    final = jnp.full((FRAMES, 1), PATCHES - 1, jnp.int32)
    return jnp.concatenate([first, inner, final], axis=1).astype(jnp.int32)


def draw_last_frame(key, part):
    key = jax.random.fold_in(key, 7)
    limit_key, order_key = jax.random.split(key)
    text_limit = jax.random.randint(limit_key, (), FRAMES, TEXT + 1, dtype=jnp.int32)
    places = jnp.arange(1, TEXT, dtype=jnp.int32)
    shuffled_ranks = jax.random.permutation(order_key, TEXT - 1).astype(jnp.int32)
    scores = jnp.where(places < text_limit, shuffled_ranks, shuffled_ranks + TEXT)
    picked_scores, picked = lax.top_k(-scores, FRAMES - 1)
    starts = places[picked.astype(jnp.int32)]
    positions = jnp.arange(TEXT, dtype=jnp.int32)
    counts = jnp.sum((starts[None, :] <= positions[:, None]).astype(jnp.int32), axis=1)
    return counts.astype(jnp.int32)


def draw_queries(key, part):
    key = jax.random.fold_in(key, 11)
    second_key = jax.random.fold_in(key, 1)
    result = jnp.clip(jax.random.normal(second_key, (TEXT, HEADS * HD), jnp.float32) * 2.5, -12.0, 12.0)
    return result.astype(jnp.bfloat16)


def steps_of(rng, shape, shards, low, largest):
    factor_of = 1.0
    for dim, shards_of in shards:
        steps = jax.random.uniform(jax.random.fold_in(jax.random.fold_in(rng, 6), dim), (shards_of,), jnp.float32, low / len(shards), largest / len(shards))
        factor_of = factor_of * jnp.repeat(jnp.exp(steps), shape[dim] // shards_of).reshape((-1,) + (1,) * (len(shape) - 1 - dim))
    return factor_of


def noise(stream_key, shape, deviation, limit, shards=(), kind=jnp.bfloat16):
    values = deviation * jax.random.normal(stream_key, shape, jnp.float32)
    if shards:
        values = values * steps_of(stream_key, shape, shards, -0.22, 0.18)
    return jnp.clip(values, -limit, limit).astype(kind)


def setup_inputs(seed: int = 0) -> dict:
    key_list = jax.random.split(jax.random.key(seed), 8)
    return {
        "vision": noise(key_list[0], (FRAMES, PATCHES, D), 1.0, 6.0, ((0, 16), (2, 2))),
        "kept_index": draw_kept_index(jax.random.fold_in(key_list[7], 71), 0),
        "w_key": noise(key_list[2], (D, KV_HEADS * HD), D ** -0.5, 0.0625, ((0, 2), (1, 16))),
        "w_value": noise(key_list[3], (D, KV_HEADS * HD), D ** -0.5, 0.0625, ((0, 2), (1, 16))),
        "queries": draw_queries(jax.random.fold_in(key_list[7], 71), 0),
        "last_frame": draw_last_frame(jax.random.fold_in(key_list[7], 71), 0),
        "attn_gate": jnp.clip(jax.random.uniform(key_list[6], (1,), jnp.float32, 0.3, 1.5), 0.3, 1.5),
    }


def reference(vision, kept_index, w_key, w_value, queries, last_frame, attn_gate):
    chosen = jnp.take_along_axis(vision, kept_index[:, :, None], axis=1)
    flattened = chosen.reshape(FRAMES * KEPT, D)
    key_rows = jnp.dot(flattened, w_key, preferred_element_type=jnp.float32).astype(jnp.bfloat16)
    value_rows = jnp.dot(flattened, w_value, preferred_element_type=jnp.float32).astype(jnp.bfloat16)
    key_float = key_rows.astype(jnp.float32).reshape(FRAMES * KEPT, KV_HEADS, HD)
    value_float = value_rows.astype(jnp.float32).reshape(FRAMES * KEPT, KV_HEADS, HD)
    group_size = HEADS // KV_HEADS
    frame_ids = jnp.arange(FRAMES * KEPT, dtype=jnp.int32) // KEPT
    gate_factor = jnp.tanh(attn_gate[0])
    block_rows = 64

    def attend_rows(inputs):
        query_block, last_block = inputs
        query_heads = query_block.astype(jnp.float32).reshape(block_rows, KV_HEADS, group_size, HD)
        scores = jnp.einsum("rkgd,jkd->rkgj", query_heads, key_float) * (HD ** -0.5)
        visible = frame_ids[None, :] <= last_block[:, None]
        scores = jnp.where(visible[:, None, None, :], scores, jnp.float32(-1e30))
        row_max = jnp.max(scores, axis=-1)
        exps = jnp.exp(scores - row_max[..., None])
        denominator = jnp.sum(exps, axis=-1)
        rounded = lax.optimization_barrier(exps.astype(jnp.bfloat16)).astype(jnp.float32)
        numerator = jnp.einsum("rkgj,jkd->rkgd", rounded, value_float)
        result = gate_factor * (numerator / denominator[..., None])
        return result.reshape(block_rows, HEADS * HD).astype(jnp.bfloat16)

    blocks = TEXT // block_rows
    outputs = lax.map(attend_rows, (queries.reshape(blocks, block_rows, HEADS * HD), last_frame.reshape(blocks, block_rows)))
    return outputs.reshape(TEXT, HEADS * HD)
```

```python
import jax
import jax.numpy as jnp
from jax import lax
from jax.experimental import pallas as pl
from jax.experimental.pallas import tpu as pltpu
from jax.sharding import PartitionSpec as P

HD = 128
MESH = pl.DeviceIdType.MESH
PIECES = 8
STACK = 2


def fused_kernel(
    vision_ref, tail_ref, index_ref, w_key_ref, w_value_ref, q_ref, last_ref, gate_ref, out_ref,
    vision_buf, onehot, chosen, weights, sums, partner_sums, kv, q_all, last_all, bias, out_parts,
    vision_sem, w_send, w_recv, c_send, c_recv, q_send, q_recv, l_send, l_recv,
    s_send, s_recv, kv_send, kv_recv, o_send, o_recv,
):
    blk = lax.axis_index("blk")
    side = lax.axis_index("head")
    z1, member, x = blk // 8, (blk % 8) // 2, blk % 2
    z0, y = member // 2, member % 2
    frame_at = lambda zz, mm, xx: zz * 8 + mm * 2 + xx
    to_x = (frame_at(z1, member, 1 - x), side)
    to_z1 = (frame_at(1 - z1, member, x), side)
    to_y = (frame_at(z1, z0 * 2 + 1 - y, x), side)
    to_z0 = (frame_at(z1, (1 - z0) * 2 + y, x), side)
    to_diagonal = (frame_at(z1, (1 - z0) * 2 + 1 - y, x), side)
    to_core = (blk, 1 - side)
    partners = (to_x, to_z1, to_y, to_z0, to_diagonal, to_core)

    def send(src, dst, send_sem, recv_sem, device):
        return pltpu.make_async_remote_copy(
            src_ref=src, dst_ref=dst, send_sem=send_sem, recv_sem=recv_sem,
            device_id=device, device_id_type=MESH,
        )

    depth = chosen.shape[3]
    main_rows = vision_buf.shape[1]

    def vision_copy(k):
        columns = pl.ds(pl.multiple_of(k * depth, depth), depth)
        slot = lax.rem(k, 2)
        return pltpu.make_async_copy(
            vision_ref.at[0, pl.ds(0, main_rows), columns], vision_buf.at[slot], vision_sem.at[slot]
        )

    def w_copy(kind, k):
        slot = weights.at[k, z1 if kind < 2 else 1 - z1, x]
        return send(slot, slot, w_send.at[kind, k], w_recv.at[kind, k], to_z1 if kind == 1 else to_x)

    def w_arrival(kind, k):
        slot = weights.at[k, z1 if kind == 0 else 1 - z1, x if kind == 1 else 1 - x]
        return send(slot, slot, w_send.at[kind, k], w_recv.at[kind, k], to_x)

    def c_copy(kind, k):
        slot = chosen.at[k, member if kind < 2 else (1 - z0) * 2 + y]
        return send(slot, slot, c_send.at[kind, k], c_recv.at[kind, k], to_z0 if kind == 1 else to_y)

    def c_arrival(kind, k):
        from_z0 = z0 if kind == 0 else 1 - z0
        from_y = y if kind == 1 else 1 - y
        slot = chosen.at[k, from_z0 * 2 + from_y]
        return send(slot, slot, c_send.at[kind, k], c_recv.at[kind, k], to_y)

    def kv_copy(kind, j):
        slot = kv.at[frame_at(z1 if kind < 2 else 1 - z1, j, x)]
        return send(slot, slot, kv_send.at[kind, j], kv_recv.at[kind, j], to_z1 if kind == 1 else to_x)

    def kv_arrival(kind, j):
        slot = kv.at[frame_at(z1 if kind == 0 else 1 - z1, j, x if kind == 1 else 1 - x)]
        return send(slot, slot, kv_send.at[kind, j], kv_recv.at[kind, j], to_x)

    width = q_all.shape[2]

    def peer(t):
        return lax.rem(member + t, 4)

    def columns_of(m):
        return pl.ds(pl.multiple_of(m * width, width), width)

    def q_copy(t):
        target = (frame_at(z1, peer(t), x), side)
        return send(q_ref.at[:, columns_of(peer(t))], q_all.at[member], q_send.at[t], q_recv.at[t], target)

    def q_arrival(t):
        slot = q_all.at[peer(4 - t)]
        return send(slot, slot, q_send.at[t], q_recv.at[t], to_y)

    def l_copy(t):
        target = (frame_at(z1, peer(t), x), side)
        return send(last_all.at[member], last_all.at[member], l_send.at[t], l_recv.at[t], target)

    def l_arrival(t):
        slot = last_all.at[peer(4 - t)]
        return send(slot, slot, l_send.at[t], l_recv.at[t], to_y)

    def o_copy(t):
        target = (frame_at(z1, peer(t), x), side)
        return send(out_parts.at[t], out_ref.at[:, columns_of(member)], o_send.at[t], o_recv.at[t], target)

    def o_arrival(t):
        slot = out_ref.at[:, columns_of(peer(4 - t))]
        return send(slot, slot, o_send.at[t], o_recv.at[t], to_y)

    def s_copy(j):
        return send(sums.at[1 - side, j], partner_sums.at[j], s_send.at[j], s_recv.at[j], to_core)

    vision_copy(0).start()
    vision_copy(1).start()

    def join_weights(k, carry):
        rows = pl.ds(pl.multiple_of(k * depth, depth), depth)
        weights[k, z1, x] = jnp.concatenate([w_key_ref[rows, :], w_value_ref[rows, :]], axis=1)
        return carry

    lax.fori_loop(0, PIECES, join_weights, 0)

    barrier = pltpu.get_barrier_semaphore()
    for device in partners:
        pl.semaphore_signal(barrier, inc=1, device_id=device, device_id_type=MESH)
    pl.semaphore_wait(barrier, len(partners))

    def send_weights(k, carry):
        w_copy(1, k).start()
        w_copy(0, k).start()
        return carry

    lax.fori_loop(0, PIECES, send_weights, 0)

    index_rows = jnp.broadcast_to(index_ref[...], (HD, HD)).T
    lanes = lax.broadcasted_iota(jnp.int32, (HD, HD), 1)
    for block in range(main_rows // HD):
        onehot[:, block * HD:(block + 1) * HD] = jnp.where(
            index_rows == lanes + block * HD, 1.0, 0.0
        ).astype(jnp.bfloat16)
    tail_start = vision_ref.shape[1] - HD
    tail_rows = lanes + tail_start
    onehot[:, main_rows:] = jnp.where(
        (index_rows == tail_rows) & (tail_rows >= main_rows), 1.0, 0.0
    ).astype(jnp.bfloat16)

    def choose(k, carry):
        vision_copy(k).wait()
        columns = pl.ds(pl.multiple_of(k * depth, depth), depth)
        picked = jnp.dot(
            onehot[:, :main_rows], vision_buf[lax.rem(k, 2)], preferred_element_type=jnp.float32
        ) + jnp.dot(
            onehot[:, main_rows:], tail_ref[:, columns], preferred_element_type=jnp.float32
        )
        chosen[k, member] = picked.astype(jnp.bfloat16)
        c_copy(1, k).start()
        c_copy(0, k).start()

        @pl.when(k + 2 < PIECES)
        def _():
            vision_copy(k + 2).start()

        return carry

    lax.fori_loop(0, PIECES, choose, 0)

    last_all[member] = jnp.broadcast_to(last_ref[...], (8, HD))
    q_all[member] = q_ref[:, columns_of(member)]
    for t in (1, 2, 3):
        l_copy(t).start()
        q_copy(t).start()

    def relay(k, carry):
        w_arrival(1, k).wait_recv()
        w_copy(2, k).start()
        c_arrival(1, k).wait_recv()
        c_copy(2, k).start()
        return carry

    lax.fori_loop(0, PIECES, relay, 0)

    sums[...] = jnp.zeros_like(sums)

    def project(k, carry):
        for kind in (0, 2):
            w_arrival(kind, k).wait_recv()
            c_arrival(kind, k).wait_recv()
        rows = chosen[k].reshape(4 * HD, depth)
        for group in range(2):
            columns = jnp.concatenate([weights[k, group, 0], weights[k, group, 1]], axis=1)
            added = jnp.dot(rows, columns, preferred_element_type=jnp.float32)
            sums[group] += added.reshape(4, HD, 2 * HD)
        return carry

    lax.fori_loop(0, PIECES, project, 0)

    for j in range(4):
        s_copy(j).start()
    for j in range(4):
        s_copy(j).wait_recv()
        total = sums[side, j] + partner_sums[j]
        key_rows = jnp.concatenate([total[:, :64], total[:, 128:192]], axis=1)
        value_rows = jnp.concatenate([total[:, 64:128], total[:, 192:]], axis=1)
        frame = frame_at(z1, j, x)
        kv[frame, 0] = key_rows.T.astype(jnp.bfloat16)
        kv[frame, 1] = value_rows.astype(jnp.bfloat16)
        kv_copy(1, j).start()
        kv_copy(0, j).start()
    for j in range(4):
        kv_arrival(1, j).wait_recv()
        kv_copy(2, j).start()
    for t in (1, 2, 3):
        l_arrival(t).wait_recv()
        q_arrival(t).wait_recv()
    for j in range(4):
        kv_arrival(0, j).wait_recv()
        kv_arrival(2, j).wait_recv()

    frames = kv.shape[0]
    keys = frames * HD
    gate = jnp.tanh(jnp.full((1, HD), gate_ref[0], jnp.float32))
    factor = HD ** (-0.5) * 1.4426950408889634

    for t in (1, 2, 3, 0):
        last_rows = jnp.broadcast_to(last_all[peer(t), 0:1, :], (HD, HD)).T
        for frame in range(frames):
            bias[:, frame * HD:(frame + 1) * HD] = jnp.where(
                last_rows >= frame, 0.0, -1e30
            ).astype(jnp.float32)

        def heads(step, carry, t=t):
            start = pl.multiple_of(step * STACK * HD, STACK * HD)
            pair = q_all[peer(t), :, pl.ds(start, STACK * HD)]
            stacked = jnp.concatenate([pair[:, i * HD:(i + 1) * HD] for i in range(STACK)], axis=0)
            key_columns = jnp.concatenate([kv[frame, 0] for frame in range(frames)], axis=1)
            scores = jnp.dot(stacked, key_columns, preferred_element_type=jnp.float32)
            scores = (scores.reshape(STACK, HD, keys) + bias[...][None]).reshape(STACK * HD, keys)
            row_max = jnp.max(scores, axis=1, keepdims=True)
            exps = jnp.exp2((scores - row_max) * factor)
            denominator = jnp.sum(exps, axis=1, keepdims=True)
            value_rows = kv[:, 1].reshape(keys, HD)
            numerator = jnp.dot(
                exps.astype(jnp.bfloat16), value_rows, preferred_element_type=jnp.float32
            )
            result = (gate * (numerator / denominator)).astype(jnp.bfloat16)
            out_parts[t, :, pl.ds(start, STACK * HD)] = jnp.concatenate(
                [result[i * HD:(i + 1) * HD] for i in range(STACK)], axis=1
            )
            return carry

        lax.fori_loop(0, width // (STACK * HD), heads, 0)
        if t:
            o_copy(t).start()
    out_ref[:, columns_of(member)] = out_parts[0]

    def sent(k, carry):
        for kind in range(3):
            w_copy(kind, k).wait_send()
            c_copy(kind, k).wait_send()
        return carry

    lax.fori_loop(0, PIECES, sent, 0)
    for j in range(4):
        s_copy(j).wait_send()
        for kind in range(3):
            kv_copy(kind, j).wait_send()
    for t in (1, 2, 3):
        l_copy(t).wait_send()
        q_copy(t).wait_send()
        o_copy(t).wait_send()
        o_arrival(t).wait_recv()


def fused_local(vision, kept_index, w_key, w_value, queries, last_frame, attn_gate):
    patches, features = vision.shape[1:]
    rows, row_width = queries.shape
    width = row_width // 4
    depth = features // PIECES
    main_rows = (patches - 1) // HD * HD
    tail = vision[0, patches - HD:]
    vmem = pl.BlockSpec(memory_space=pltpu.VMEM)
    dma = pltpu.SemaphoreType.DMA
    return pl.pallas_call(
        fused_kernel,
        out_shape=jax.ShapeDtypeStruct(queries.shape, jnp.bfloat16),
        in_specs=[pl.BlockSpec(memory_space=pl.ANY)] + [vmem] * 6
        + [pl.BlockSpec(memory_space=pltpu.SMEM)],
        out_specs=vmem,
        scratch_shapes=[
            pltpu.VMEM((2, main_rows, depth), jnp.bfloat16),
            pltpu.VMEM((HD, main_rows + HD), jnp.bfloat16),
            pltpu.VMEM((PIECES, 4, HD, depth), jnp.bfloat16),
            pltpu.VMEM((PIECES, 2, 2, depth, HD), jnp.bfloat16),
            pltpu.VMEM((2, 4, HD, 2 * HD), jnp.float32),
            pltpu.VMEM((4, HD, 2 * HD), jnp.float32),
            pltpu.VMEM((16, 2, HD, HD), jnp.bfloat16),
            pltpu.VMEM((4, rows, width), jnp.bfloat16),
            pltpu.VMEM((4, 8, HD), jnp.int32),
            pltpu.VMEM((rows, 16 * HD), jnp.float32),
            pltpu.VMEM((4, rows, width), jnp.bfloat16),
            dma((2,)),
            dma((3, PIECES)), dma((3, PIECES)),
            dma((3, PIECES)), dma((3, PIECES)),
            dma((4,)), dma((4,)), dma((4,)), dma((4,)), dma((4,)), dma((4,)),
            dma((3, 4)), dma((3, 4)),
            dma((4,)), dma((4,)),
        ],
        compiler_params=pltpu.CompilerParams(
            collective_id=0, has_side_effects=True, vmem_limit_bytes=52 * 2**20
        ),
    )(vision, tail, kept_index, w_key, w_value, queries, last_frame.reshape(1, rows), attn_gate)


def fold_frames(running, query_heads, last_rows, key_piece, value_piece):
    row_max, denominator, numerator = running
    frames_here = key_piece.shape[0]
    scores = jnp.einsum(
        "rkgd,fjkd->rkgfj", query_heads, key_piece, preferred_element_type=jnp.float32
    ) * HD ** (-0.5)
    frame_ids = jnp.arange(frames_here, dtype=jnp.int32)
    visible = frame_ids[None, :] <= last_rows[:, None]
    scores = jnp.where(visible[:, None, None, :, None], scores, jnp.float32(-1e30))
    new_max = jnp.maximum(row_max, jnp.max(scores, axis=(3, 4)))
    exps = jnp.exp(scores - new_max[..., None, None])
    new_denominator = jnp.sum(exps, axis=(3, 4))
    weights = exps.astype(jnp.bfloat16)
    added = jnp.einsum("rkgfj,fjkd->rkgd", weights, value_piece, preferred_element_type=jnp.float32)
    return (new_max, new_denominator, added)


def attend(rows_q, rows_last, groups, key_rows, value_rows, attn_gate):
    total_rows, row_width = rows_q.shape
    local_kv = key_rows.shape[2] // HD
    group_size = row_width // HD // local_kv
    group_rows = total_rows // groups
    query_groups = [rows_q.reshape(group_rows, local_kv, group_size, HD)]
    last_groups = [rows_last]
    initial = tuple(
        (
            (
                jnp.full((group_rows, local_kv, group_size), -1e30, jnp.float32),
                jnp.zeros((group_rows, local_kv, group_size), jnp.float32),
                jnp.zeros((group_rows, local_kv, group_size, HD), jnp.float32),
            )
            for member in range(groups)
        )
    )
    key_piece = lax.all_gather(key_rows, "blk", axis=0, tiled=True)
    value_piece = lax.all_gather(value_rows, "blk", axis=0, tiled=True)
    frames_here = key_piece.shape[0]
    key_piece = key_piece.reshape(frames_here, key_piece.shape[1], local_kv, HD)
    value_piece = value_piece.reshape(frames_here, value_piece.shape[1], local_kv, HD)
    member = 0
    query_heads = query_groups[member]
    last_rows = last_groups[member]
    state_new = fold_frames(initial[member], query_heads, last_rows, key_piece, value_piece)
    updated = [state_new]
    results = tuple(updated)
    gate_factor = jnp.tanh(attn_gate[0])
    pieces_out = [
        (gate_factor * (numerator / denominator[..., None])).reshape(group_rows, row_width)
        for row_max, denominator, numerator in results
    ]
    return pieces_out[0].astype(jnp.bfloat16)


def local(vision, kept_index, w_key, w_value, queries, last_frame, attn_gate):
    chosen = vision[0][kept_index[0]]
    stacked = jnp.stack([w_key, w_value])
    partial_value = jnp.einsum(
        "td,sdc->stc",
        chosen,
        lax.all_gather(stacked, "blk", axis=2, tiled=True),
        preferred_element_type=jnp.float32,
    )
    summed = lax.psum_scatter(partial_value, "head", scatter_dimension=2, tiled=True).astype(
        jnp.bfloat16
    )
    key_rows = summed[0][None]
    value_rows = summed[1][None]
    return attend(queries, last_frame, 1, key_rows, value_rows, attn_gate)


def solution(mesh):
    in_specs = (
        P("blk", None, "head"),
        P("blk", None),
        P("head", "blk"),
        P("head", "blk"),
        P("blk", "head"),
        P("blk"),
        P(),
    )
    out_specs = P("blk", "head")
    if dict(mesh.shape) == {"blk": 16, "head": 2}:
        return jax.shard_map(
            fused_local, mesh=mesh, in_specs=in_specs, out_specs=out_specs, check_vma=False
        )
    return jax.shard_map(local, mesh=mesh, in_specs=in_specs, out_specs=out_specs, check_vma=False)
```

```python
import jax
import jax.numpy as jnp
from jax import lax
from jax.experimental import pallas as pl
from jax.experimental.pallas import tpu as pltpu
from jax.sharding import PartitionSpec as P

HD = 128
MESH = pl.DeviceIdType.MESH
PIECES = 8
STACK = 2


def fused_kernel(
    vision_ref, index_hbm, w_key_ref, w_value_ref, q_ref, last_hbm, gate_ref, out_ref,
    vision_buf, index_ref, last_ref, onehot, chosen, weights, sums, partner_sums, keys_all,
    values_all, q_all, last_all, exps_own, exps_even, exps_odd, dens_own, dens_even, dens_odd,
    out_parts, vision_sem, small_sem, load_sem,
    w_send, w_recv, c_send, c_recv, q_send, q_recv, l_send, l_recv,
    s_send, s_recv, k_send, k_recv, v_send, v_recv, o_send, o_recv,
):
    blk = lax.axis_index("blk")
    side = lax.axis_index("head")
    z1, member, x = blk // 8, (blk % 8) // 2, blk % 2
    z0, y = member // 2, member % 2
    frame_at = lambda zz, mm, xx: zz * 8 + mm * 2 + xx
    to_x = (frame_at(z1, member, 1 - x), side)
    to_z1 = (frame_at(1 - z1, member, x), side)
    to_y = (frame_at(z1, z0 * 2 + 1 - y, x), side)
    to_z0 = (frame_at(z1, (1 - z0) * 2 + y, x), side)
    to_diagonal = (frame_at(z1, (1 - z0) * 2 + 1 - y, x), side)
    to_core = (blk, 1 - side)
    partners = (to_x, to_z1, to_y, to_z0, to_diagonal, to_core)

    def send(src, dst, send_sem, recv_sem, device):
        return pltpu.make_async_remote_copy(
            src_ref=src, dst_ref=dst, send_sem=send_sem, recv_sem=recv_sem,
            device_id=device, device_id_type=MESH,
        )

    depth = chosen.shape[3]
    patches = vision_buf.shape[1]

    def vision_copy(k):
        columns = pl.ds(pl.multiple_of(k * depth, depth), depth)
        slot = lax.rem(k, 2)
        return pltpu.make_async_copy(
            vision_ref.at[0, :, columns], vision_buf.at[slot], vision_sem.at[slot]
        )

    def w_copy(kind, k):
        slot = weights.at[k, z1 if kind < 2 else 1 - z1, x]
        return send(slot, slot, w_send.at[kind, k], w_recv.at[kind, k], to_z1 if kind == 1 else to_x)

    def w_arrival(kind, k):
        slot = weights.at[k, z1 if kind == 0 else 1 - z1, x if kind == 1 else 1 - x]
        return send(slot, slot, w_send.at[kind, k], w_recv.at[kind, k], to_x)

    def c_copy(kind, k):
        slot = chosen.at[k, member if kind < 2 else (1 - z0) * 2 + y]
        return send(slot, slot, c_send.at[kind, k], c_recv.at[kind, k], to_z0 if kind == 1 else to_y)

    def c_arrival(kind, k):
        from_z0 = z0 if kind == 0 else 1 - z0
        from_y = y if kind == 1 else 1 - y
        slot = chosen.at[k, from_z0 * 2 + from_y]
        return send(slot, slot, c_send.at[kind, k], c_recv.at[kind, k], to_y)

    def kv_copy(held, send_sem, recv_sem, kind, j):
        slot = held.at[frame_at(z1 if kind < 2 else 1 - z1, j, x)]
        return send(slot, slot, send_sem.at[kind, j], recv_sem.at[kind, j], to_z1 if kind == 1 else to_x)

    def kv_arrival(held, send_sem, recv_sem, kind, j):
        slot = held.at[frame_at(z1 if kind == 0 else 1 - z1, j, x if kind == 1 else 1 - x)]
        return send(slot, slot, send_sem.at[kind, j], recv_sem.at[kind, j], to_x)

    key_part = (keys_all, k_send, k_recv)
    value_part = (values_all, v_send, v_recv)

    width = q_all.shape[2]

    def peer(t):
        return lax.rem(member + t, 4)

    def columns_of(m):
        return pl.ds(pl.multiple_of(m * width, width), width)

    def q_copy(t):
        target = (frame_at(z1, peer(t), x), side)
        return send(q_ref.at[:, columns_of(peer(t))], q_all.at[member], q_send.at[t], q_recv.at[t], target)

    def q_arrival(t):
        slot = q_all.at[peer(4 - t)]
        return send(slot, slot, q_send.at[t], q_recv.at[t], to_y)

    def l_copy(t):
        target = (frame_at(z1, peer(t), x), side)
        return send(last_all.at[member], last_all.at[member], l_send.at[t], l_recv.at[t], target)

    def l_arrival(t):
        slot = last_all.at[peer(4 - t)]
        return send(slot, slot, l_send.at[t], l_recv.at[t], to_y)

    def o_copy(t):
        target = (frame_at(z1, peer(t), x), side)
        return send(out_parts.at[t], out_ref.at[:, columns_of(member)], o_send.at[t], o_recv.at[t], target)

    def o_arrival(t):
        slot = out_ref.at[:, columns_of(peer(4 - t))]
        return send(slot, slot, o_send.at[t], o_recv.at[t], to_y)

    def s_copy(j):
        return send(sums.at[1 - side, j], partner_sums.at[j], s_send.at[j], s_recv.at[j], to_core)

    def w_load(which, k):
        columns = pl.ds(pl.multiple_of(k * depth, depth), depth)
        return pltpu.make_async_copy(
            (w_key_ref, w_value_ref)[which].at[:, columns],
            weights.at[k, z1, x, pl.ds(which * 64, 64)], load_sem.at[which, k],
        )

    own_q = pltpu.make_async_copy(q_ref.at[:, columns_of(member)], q_all.at[member], small_sem.at[0])
    index_copy = pltpu.make_async_copy(index_hbm, index_ref, small_sem.at[1])
    last_copy = pltpu.make_async_copy(last_hbm, last_ref, small_sem.at[2])

    barrier = pltpu.get_barrier_semaphore()
    for device in partners:
        pl.semaphore_signal(barrier, inc=1, device_id=device, device_id_type=MESH)

    def load_weights(k, carry):
        w_load(0, k).start()
        w_load(1, k).start()
        return carry

    index_copy.start()
    last_copy.start()
    lax.fori_loop(0, PIECES, load_weights, 0)
    vision_copy(0).start()
    vision_copy(1).start()
    own_q.start()
    pl.semaphore_wait(barrier, len(partners))

    def send_weights(k, carry):
        w_load(0, k).wait()
        w_load(1, k).wait()
        w_copy(1, k).start()
        w_copy(0, k).start()
        return carry

    lax.fori_loop(0, PIECES, send_weights, 0)

    index_copy.wait()
    last_copy.wait()
    index_rows = jnp.broadcast_to(index_ref[...], (HD, HD)).T
    lanes = lax.broadcasted_iota(jnp.int32, (HD, HD), 1)
    for start in range(0, patches, HD):
        stop = min(start + HD, patches)
        onehot[:, start:stop] = jnp.where(index_rows == lanes + start, 1.0, 0.0).astype(
            jnp.bfloat16
        )[:, :stop - start]

    def choose(k, carry):
        vision_copy(k).wait()
        picked = jnp.dot(
            onehot[...], vision_buf[lax.rem(k, 2)], preferred_element_type=jnp.float32
        )
        chosen[k, member] = picked.astype(jnp.bfloat16)
        c_copy(1, k).start()
        c_copy(0, k).start()

        @pl.when(k + 2 < PIECES)
        def _():
            vision_copy(k + 2).start()

        return carry

    lax.fori_loop(0, PIECES, choose, 0)

    def relay(k, carry):
        w_arrival(1, k).wait_recv()
        w_copy(2, k).start()
        c_arrival(1, k).wait_recv()
        c_copy(2, k).start()
        return carry

    lax.fori_loop(0, PIECES, relay, 0)

    last_all[member] = jnp.broadcast_to(last_ref[...], (8, HD))
    for t in (1, 2, 3):
        l_copy(t).start()
        q_copy(t).start()

    sums[...] = jnp.zeros_like(sums)

    def project(k, carry):
        for kind in (0, 2):
            w_arrival(kind, k).wait_recv()
            c_arrival(kind, k).wait_recv()
        rows = chosen[k].reshape(4 * HD, depth)
        for group in range(2):
            columns = weights[k, group].reshape(2 * HD, depth)
            added = lax.dot_general(
                rows, columns, (((1,), (1,)), ((), ())), preferred_element_type=jnp.float32
            )
            sums[group] += added.reshape(4, HD, 2 * HD)
        return carry

    lax.fori_loop(0, PIECES, project, 0)

    for j in range(4):
        s_copy(j).start()
    for j in range(4):
        s_copy(j).wait_recv()
        total = sums[side, j] + partner_sums[j]
        key_rows = jnp.concatenate([total[:, :64], total[:, 128:192]], axis=1)
        value_rows = jnp.concatenate([total[:, 64:128], total[:, 192:]], axis=1)
        frame = frame_at(z1, j, x)
        keys_all[frame] = key_rows.T.astype(jnp.bfloat16)
        values_all[frame] = value_rows.astype(jnp.bfloat16)
        kv_copy(*key_part, 1, j).start()
        kv_copy(*key_part, 0, j).start()
    for j in range(4):
        kv_copy(*value_part, 1, j).start()
        kv_copy(*value_part, 0, j).start()
    for part in (key_part, value_part):
        for j in range(4):
            kv_arrival(*part, 1, j).wait_recv()
            kv_copy(*part, 2, j).start()
    own_q.wait()
    for j in range(4):
        kv_arrival(*key_part, 0, j).wait_recv()
        kv_arrival(*key_part, 2, j).wait_recv()

    frames = keys_all.shape[0]
    keys = frames * HD
    gate = jnp.tanh(jnp.full((1, HD), gate_ref[0], jnp.float32))
    factor = HD ** (-0.5) * 1.4426950408889634
    steps = width // (STACK * HD)
    feature = lax.broadcasted_iota(jnp.int32, (HD, HD), 0)

    def hidden_of(t):
        last_rows = jnp.broadcast_to(last_all[peer(t), 0:1, :], (HD, HD)).T
        hidden = jnp.where(last_rows < lanes, -1e30, 0.0).astype(jnp.bfloat16)
        return jnp.concatenate([hidden] * STACK, axis=0)

    def weigh(t, hidden, step, exps_ref, dens_ref):
        start = pl.multiple_of(step * STACK * HD, STACK * HD)
        heads = q_all[peer(t), :, pl.ds(start, STACK * HD)]
        stacked = jnp.concatenate([heads[:, i * HD:(i + 1) * HD] for i in range(STACK)], axis=0)
        key_columns = jnp.concatenate([keys_all[frame] for frame in range(frames)], axis=1)
        marks = jnp.concatenate(
            [jnp.where(feature == frame, 1.0, 0.0).astype(jnp.bfloat16) for frame in range(frames)],
            axis=1,
        )
        scores = jnp.dot(
            jnp.concatenate([stacked, hidden], axis=1),
            jnp.concatenate([key_columns, marks], axis=0),
            preferred_element_type=jnp.float32,
        )
        row_max = jnp.max(scores, axis=1, keepdims=True)
        exps = jnp.exp2((scores - row_max) * factor)
        dens_ref[step] = jnp.broadcast_to(jnp.sum(exps, axis=1, keepdims=True), (STACK * HD, HD))
        exps_ref[step] = exps.astype(jnp.bfloat16)

    def combine(t, step, exps_ref, dens_ref):
        start = pl.multiple_of(step * STACK * HD, STACK * HD)
        value_rows = values_all[...].reshape(keys, HD)
        numerator = jnp.dot(exps_ref[step], value_rows, preferred_element_type=jnp.float32)
        result = (gate * (numerator / dens_ref[step])).astype(jnp.bfloat16)
        out_parts[t, :, pl.ds(start, STACK * HD)] = jnp.concatenate(
            [result[i * HD:(i + 1) * HD] for i in range(STACK)], axis=1
        )

    def run(weighed, combined):
        hidden = hidden_of(weighed[0]) if weighed else None

        def body(step, carry):
            if combined:
                combine(combined[0], step, *combined[1])
            if weighed:
                weigh(weighed[0], hidden, step, *weighed[1])
            return carry

        lax.fori_loop(0, steps, body, 0)

    own, even, odd = (exps_own, dens_own), (exps_even, dens_even), (exps_odd, dens_odd)
    run((0, own), None)
    for t in (1, 2, 3):
        l_arrival(t).wait_recv()
        q_arrival(t).wait_recv()
    run((2, even), None)
    for j in range(4):
        kv_arrival(*value_part, 0, j).wait_recv()
        kv_arrival(*value_part, 2, j).wait_recv()
    run((1, odd), (2, even))
    o_copy(2).start()
    run((3, even), (1, odd))
    o_copy(1).start()
    run(None, (3, even))
    o_copy(3).start()
    run(None, (0, own))
    out_ref[:, columns_of(member)] = out_parts[0]

    def sent(k, carry):
        for kind in range(3):
            w_copy(kind, k).wait_send()
            c_copy(kind, k).wait_send()
        return carry

    lax.fori_loop(0, PIECES, sent, 0)
    for j in range(4):
        s_copy(j).wait_send()
        for kind in range(3):
            kv_copy(*key_part, kind, j).wait_send()
            kv_copy(*value_part, kind, j).wait_send()
    for t in (1, 2, 3):
        l_copy(t).wait_send()
        q_copy(t).wait_send()
        o_copy(t).wait_send()
        o_arrival(t).wait_recv()


def fused_local(vision, kept_index, w_key, w_value, queries, last_frame, attn_gate):
    patches, features = vision.shape[1:]
    rows, row_width = queries.shape
    width = row_width // 4
    depth = features // PIECES
    steps = width // (STACK * HD)
    vmem = pltpu.VMEM
    dma = pltpu.SemaphoreType.DMA
    exps = vmem((steps, STACK * HD, 16 * HD), jnp.bfloat16)
    dens = vmem((steps, STACK * HD, HD), jnp.float32)
    return pl.pallas_call(
        fused_kernel,
        out_shape=jax.ShapeDtypeStruct(queries.shape, jnp.bfloat16),
        in_specs=[pl.BlockSpec(memory_space=pl.ANY)] * 6 + [pl.BlockSpec(memory_space=pltpu.SMEM)],
        out_specs=pl.BlockSpec(memory_space=vmem),
        scratch_shapes=[
            vmem((2, patches, depth), jnp.bfloat16),
            vmem((1, HD), jnp.int32),
            vmem((1, rows), jnp.int32),
            vmem((HD, patches), jnp.bfloat16),
            vmem((PIECES, 4, HD, depth), jnp.bfloat16),
            vmem((PIECES, 2, 2, HD, depth), jnp.bfloat16),
            vmem((2, 4, HD, 2 * HD), jnp.float32),
            vmem((4, HD, 2 * HD), jnp.float32),
            vmem((16, HD, HD), jnp.bfloat16),
            vmem((16, HD, HD), jnp.bfloat16),
            vmem((4, rows, width), jnp.bfloat16),
            vmem((4, 8, HD), jnp.int32),
            exps, exps, exps, dens, dens, dens,
            vmem((4, rows, width), jnp.bfloat16),
            dma((2,)), dma((3,)), dma((2, PIECES)),
            dma((3, PIECES)), dma((3, PIECES)),
            dma((3, PIECES)), dma((3, PIECES)),
            dma((4,)), dma((4,)), dma((4,)), dma((4,)), dma((4,)), dma((4,)),
            dma((3, 4)), dma((3, 4)), dma((3, 4)), dma((3, 4)),
            dma((4,)), dma((4,)),
        ],
        compiler_params=pltpu.CompilerParams(
            collective_id=0, has_side_effects=True, vmem_limit_bytes=56 * 2**20
        ),
    )(vision, kept_index, w_key.T, w_value.T, queries, last_frame.reshape(1, rows), attn_gate)


def fold_frames(running, query_heads, last_rows, key_piece, value_piece):
    row_max, denominator, numerator = running
    frames_here = key_piece.shape[0]
    scores = jnp.einsum(
        "rkgd,fjkd->rkgfj", query_heads, key_piece, preferred_element_type=jnp.float32
    ) * HD ** (-0.5)
    frame_ids = jnp.arange(frames_here, dtype=jnp.int32)
    visible = frame_ids[None, :] <= last_rows[:, None]
    scores = jnp.where(visible[:, None, None, :, None], scores, jnp.float32(-1e30))
    new_max = jnp.maximum(row_max, jnp.max(scores, axis=(3, 4)))
    exps = jnp.exp(scores - new_max[..., None, None])
    new_denominator = jnp.sum(exps, axis=(3, 4))
    weights = exps.astype(jnp.bfloat16)
    added = jnp.einsum("rkgfj,fjkd->rkgd", weights, value_piece, preferred_element_type=jnp.float32)
    return (new_max, new_denominator, added)


def attend(rows_q, rows_last, groups, key_rows, value_rows, attn_gate):
    total_rows, row_width = rows_q.shape
    local_kv = key_rows.shape[2] // HD
    group_size = row_width // HD // local_kv
    group_rows = total_rows // groups
    query_groups = [rows_q.reshape(group_rows, local_kv, group_size, HD)]
    last_groups = [rows_last]
    initial = tuple(
        (
            (
                jnp.full((group_rows, local_kv, group_size), -1e30, jnp.float32),
                jnp.zeros((group_rows, local_kv, group_size), jnp.float32),
                jnp.zeros((group_rows, local_kv, group_size, HD), jnp.float32),
            )
            for member in range(groups)
        )
    )
    key_piece = lax.all_gather(key_rows, "blk", axis=0, tiled=True)
    value_piece = lax.all_gather(value_rows, "blk", axis=0, tiled=True)
    frames_here = key_piece.shape[0]
    key_piece = key_piece.reshape(frames_here, key_piece.shape[1], local_kv, HD)
    value_piece = value_piece.reshape(frames_here, value_piece.shape[1], local_kv, HD)
    member = 0
    query_heads = query_groups[member]
    last_rows = last_groups[member]
    state_new = fold_frames(initial[member], query_heads, last_rows, key_piece, value_piece)
    updated = [state_new]
    results = tuple(updated)
    gate_factor = jnp.tanh(attn_gate[0])
    pieces_out = [
        (gate_factor * (numerator / denominator[..., None])).reshape(group_rows, row_width)
        for row_max, denominator, numerator in results
    ]
    return pieces_out[0].astype(jnp.bfloat16)


def local(vision, kept_index, w_key, w_value, queries, last_frame, attn_gate):
    chosen = vision[0][kept_index[0]]
    stacked = jnp.stack([w_key, w_value])
    partial_value = jnp.einsum(
        "td,sdc->stc",
        chosen,
        lax.all_gather(stacked, "blk", axis=2, tiled=True),
        preferred_element_type=jnp.float32,
    )
    summed = lax.psum_scatter(partial_value, "head", scatter_dimension=2, tiled=True).astype(
        jnp.bfloat16
    )
    key_rows = summed[0][None]
    value_rows = summed[1][None]
    return attend(queries, last_frame, 1, key_rows, value_rows, attn_gate)


def solution(mesh):
    in_specs = (
        P("blk", None, "head"),
        P("blk", None),
        P("head", "blk"),
        P("head", "blk"),
        P("blk", "head"),
        P("blk"),
        P(),
    )
    out_specs = P("blk", "head")
    if dict(mesh.shape) == {"blk": 16, "head": 2}:
        return jax.shard_map(
            fused_local, mesh=mesh, in_specs=in_specs, out_specs=out_specs, check_vma=False
        )
    return jax.shard_map(local, mesh=mesh, in_specs=in_specs, out_specs=out_specs, check_vma=False)
```

```python
import jax
import jax.numpy as jnp
from jax import lax
from jax.experimental import pallas as pl
from jax.experimental.pallas import tpu as pltpu
from jax.sharding import PartitionSpec as P

HD = 128
MESH = pl.DeviceIdType.MESH
PIECES = 8
LAG = 3
STACK = 2


def fused_kernel(
    vision_ref, index_hbm, w_key_ref, w_value_ref, q_ref, last_hbm, gate_ref, out_ref,
    vision_buf, index_ref, last_ref, onehot, chosen, weights, sums, partner_sums, keys_all,
    values_all, q_all, last_all, exps_own, exps_even, exps_odd, dens_own, dens_even, dens_odd,
    out_parts, vision_sem, small_sem, load_sem,
    w_send, w_recv, c_send, c_recv, q_send, q_recv, l_send, l_recv,
    s_send, s_recv, k_send, k_recv, v_send, v_recv, o_send, o_recv,
):
    blk = lax.axis_index("blk")
    side = lax.axis_index("head")
    z1, member, x = blk // 8, (blk % 8) // 2, blk % 2
    z0, y = member // 2, member % 2
    frame_at = lambda zz, mm, xx: zz * 8 + mm * 2 + xx
    to_x = (frame_at(z1, member, 1 - x), side)
    to_z1 = (frame_at(1 - z1, member, x), side)
    to_y = (frame_at(z1, z0 * 2 + 1 - y, x), side)
    to_z0 = (frame_at(z1, (1 - z0) * 2 + y, x), side)
    to_diagonal = (frame_at(z1, (1 - z0) * 2 + 1 - y, x), side)
    to_core = (blk, 1 - side)
    partners = (to_x, to_z1, to_y, to_z0, to_diagonal, to_core)

    def send(src, dst, send_sem, recv_sem, device):
        return pltpu.make_async_remote_copy(
            src_ref=src, dst_ref=dst, send_sem=send_sem, recv_sem=recv_sem,
            device_id=device, device_id_type=MESH,
        )

    depth = chosen.shape[3]
    patches = vision_buf.shape[1]

    def vision_copy(k):
        columns = pl.ds(pl.multiple_of(k * depth, depth), depth)
        slot = lax.rem(k, 2)
        return pltpu.make_async_copy(
            vision_ref.at[0, :, columns], vision_buf.at[slot], vision_sem.at[slot]
        )

    def w_copy(kind, k):
        slot = weights.at[k, z1 if kind < 2 else 1 - z1, x]
        return send(slot, slot, w_send.at[kind, k], w_recv.at[kind, k], to_z1 if kind == 1 else to_x)

    def w_arrival(kind, k):
        slot = weights.at[k, z1 if kind == 0 else 1 - z1, x if kind == 1 else 1 - x]
        return send(slot, slot, w_send.at[kind, k], w_recv.at[kind, k], to_x)

    def c_copy(kind, k):
        slot = chosen.at[k, member if kind < 2 else (1 - z0) * 2 + y]
        return send(slot, slot, c_send.at[kind, k], c_recv.at[kind, k], to_z0 if kind == 1 else to_y)

    def c_arrival(kind, k):
        from_z0 = z0 if kind == 0 else 1 - z0
        from_y = y if kind == 1 else 1 - y
        slot = chosen.at[k, from_z0 * 2 + from_y]
        return send(slot, slot, c_send.at[kind, k], c_recv.at[kind, k], to_y)

    def kv_copy(held, send_sem, recv_sem, kind, j):
        slot = held.at[frame_at(z1 if kind < 2 else 1 - z1, j, x)]
        return send(slot, slot, send_sem.at[kind, j], recv_sem.at[kind, j], to_z1 if kind == 1 else to_x)

    def kv_arrival(held, send_sem, recv_sem, kind, j):
        slot = held.at[frame_at(z1 if kind == 0 else 1 - z1, j, x if kind == 1 else 1 - x)]
        return send(slot, slot, send_sem.at[kind, j], recv_sem.at[kind, j], to_x)

    key_part = (keys_all, k_send, k_recv)
    value_part = (values_all, v_send, v_recv)

    width = q_all.shape[2]

    def peer(t):
        return lax.rem(member + t, 4)

    def columns_of(m):
        return pl.ds(pl.multiple_of(m * width, width), width)

    def q_copy(t):
        target = (frame_at(z1, peer(t), x), side)
        return send(q_ref.at[:, columns_of(peer(t))], q_all.at[member], q_send.at[t], q_recv.at[t], target)

    def q_arrival(t):
        slot = q_all.at[peer(4 - t)]
        return send(slot, slot, q_send.at[t], q_recv.at[t], to_y)

    def l_copy(t):
        target = (frame_at(z1, peer(t), x), side)
        return send(last_all.at[member], last_all.at[member], l_send.at[t], l_recv.at[t], target)

    def l_arrival(t):
        slot = last_all.at[peer(4 - t)]
        return send(slot, slot, l_send.at[t], l_recv.at[t], to_y)

    def o_copy(t):
        target = (frame_at(z1, peer(t), x), side)
        return send(out_parts.at[t], out_ref.at[:, columns_of(member)], o_send.at[t], o_recv.at[t], target)

    def o_arrival(t):
        slot = out_ref.at[:, columns_of(peer(4 - t))]
        return send(slot, slot, o_send.at[t], o_recv.at[t], to_y)

    def s_copy(j):
        return send(sums.at[1 - side, j], partner_sums.at[j], s_send.at[j], s_recv.at[j], to_core)

    def w_load(which, k):
        columns = pl.ds(pl.multiple_of(k * depth, depth), depth)
        return pltpu.make_async_copy(
            (w_key_ref, w_value_ref)[which].at[:, columns],
            weights.at[k, z1, x, pl.ds(which * 64, 64)], load_sem.at[which, k],
        )

    own_q = pltpu.make_async_copy(q_ref.at[:, columns_of(member)], q_all.at[member], small_sem.at[0])
    index_copy = pltpu.make_async_copy(index_hbm, index_ref, small_sem.at[1])
    last_copy = pltpu.make_async_copy(last_hbm, last_ref, small_sem.at[2])

    barrier = pltpu.get_barrier_semaphore()
    for device in partners:
        pl.semaphore_signal(barrier, inc=1, device_id=device, device_id_type=MESH)

    def load_weights(k, carry):
        w_load(0, k).start()
        w_load(1, k).start()
        return carry

    index_copy.start()
    last_copy.start()
    lax.fori_loop(0, PIECES, load_weights, 0)
    vision_copy(0).start()
    vision_copy(1).start()
    own_q.start()
    pl.semaphore_wait(barrier, len(partners))

    def send_weights(k, carry):
        w_load(0, k).wait()
        w_load(1, k).wait()
        w_copy(1, k).start()
        w_copy(0, k).start()
        return carry

    lax.fori_loop(0, PIECES, send_weights, 0)

    index_copy.wait()
    last_copy.wait()
    index_rows = jnp.broadcast_to(index_ref[...], (HD, HD)).T
    lanes = lax.broadcasted_iota(jnp.int32, (HD, HD), 1)
    for start in range(0, patches, HD):
        stop = min(start + HD, patches)
        onehot[:, start:stop] = jnp.where(index_rows == lanes + start, 1.0, 0.0).astype(
            jnp.bfloat16
        )[:, :stop - start]

    def choose(k, carry):
        vision_copy(k).wait()
        picked = jnp.dot(
            onehot[...], vision_buf[lax.rem(k, 2)], preferred_element_type=jnp.float32
        )
        chosen[k, member] = picked.astype(jnp.bfloat16)
        c_copy(1, k).start()
        c_copy(0, k).start()

        @pl.when(k + 2 < PIECES)
        def _():
            vision_copy(k + 2).start()

        return carry

    lax.fori_loop(0, PIECES, choose, 0)

    last_all[member] = jnp.broadcast_to(last_ref[...], (8, HD))
    sums[...] = jnp.zeros_like(sums)

    def project(k):
        for kind in (0, 2):
            w_arrival(kind, k).wait_recv()
            c_arrival(kind, k).wait_recv()
        rows = chosen[k].reshape(4 * HD, depth)
        for group in range(2):
            columns = weights[k, group].reshape(2 * HD, depth)
            added = lax.dot_general(
                rows, columns, (((1,), (1,)), ((), ())), preferred_element_type=jnp.float32
            )
            sums[group] += added.reshape(4, HD, 2 * HD)

    def relay_and_project(k, carry):
        @pl.when(k < PIECES)
        def _():
            w_arrival(1, k).wait_recv()
            w_copy(2, k).start()
            c_arrival(1, k).wait_recv()
            c_copy(2, k).start()

        @pl.when(k == PIECES - 1)
        def _():
            for t in (1, 2, 3):
                l_copy(t).start()
                q_copy(t).start()

        @pl.when(k >= LAG)
        def _():
            project(k - LAG)

        return carry

    lax.fori_loop(0, PIECES + LAG, relay_and_project, 0)

    for j in range(4):
        s_copy(j).start()
    for j in range(4):
        s_copy(j).wait_recv()
        total = sums[side, j] + partner_sums[j]
        key_rows = jnp.concatenate([total[:, :64], total[:, 128:192]], axis=1)
        value_rows = jnp.concatenate([total[:, 64:128], total[:, 192:]], axis=1)
        frame = frame_at(z1, j, x)
        keys_all[frame] = key_rows.T.astype(jnp.bfloat16)
        values_all[frame] = value_rows.astype(jnp.bfloat16)
        kv_copy(*key_part, 1, j).start()
        kv_copy(*key_part, 0, j).start()
    for j in range(4):
        kv_copy(*value_part, 1, j).start()
    for j in range(4):
        kv_arrival(*key_part, 1, j).wait_recv()
        kv_copy(*key_part, 2, j).start()
    for j in range(4):
        kv_copy(*value_part, 0, j).start()
    for j in range(4):
        kv_arrival(*value_part, 1, j).wait_recv()
        kv_copy(*value_part, 2, j).start()
    own_q.wait()
    for j in range(4):
        kv_arrival(*key_part, 0, j).wait_recv()
        kv_arrival(*key_part, 2, j).wait_recv()

    frames = keys_all.shape[0]
    keys = frames * HD
    gate = jnp.tanh(jnp.full((1, HD), gate_ref[0], jnp.float32))
    factor = HD ** (-0.5) * 1.4426950408889634
    steps = width // (STACK * HD)
    feature = lax.broadcasted_iota(jnp.int32, (HD, HD), 0)

    def hidden_of(t):
        last_rows = jnp.broadcast_to(last_all[peer(t), 0:1, :], (HD, HD)).T
        hidden = jnp.where(last_rows < lanes, -1e30, 0.0).astype(jnp.bfloat16)
        return jnp.concatenate([hidden] * STACK, axis=0)

    def weigh(t, hidden, step, exps_ref, dens_ref):
        start = pl.multiple_of(step * STACK * HD, STACK * HD)
        heads = q_all[peer(t), :, pl.ds(start, STACK * HD)]
        stacked = jnp.concatenate([heads[:, i * HD:(i + 1) * HD] for i in range(STACK)], axis=0)
        key_columns = jnp.concatenate([keys_all[frame] for frame in range(frames)], axis=1)
        marks = jnp.concatenate(
            [jnp.where(feature == frame, 1.0, 0.0).astype(jnp.bfloat16) for frame in range(frames)],
            axis=1,
        )
        scores = jnp.dot(
            jnp.concatenate([stacked, hidden], axis=1),
            jnp.concatenate([key_columns, marks], axis=0),
            preferred_element_type=jnp.float32,
        )
        row_max = jnp.max(scores, axis=1, keepdims=True)
        exps = jnp.exp2((scores - row_max) * factor)
        dens_ref[step] = jnp.broadcast_to(jnp.sum(exps, axis=1, keepdims=True), (STACK * HD, HD))
        exps_ref[step] = exps.astype(jnp.bfloat16)

    def combine(t, step, exps_ref, dens_ref):
        start = pl.multiple_of(step * STACK * HD, STACK * HD)
        value_rows = values_all[...].reshape(keys, HD)
        numerator = jnp.dot(exps_ref[step], value_rows, preferred_element_type=jnp.float32)
        result = (gate * (numerator / dens_ref[step])).astype(jnp.bfloat16)
        out_parts[t, :, pl.ds(start, STACK * HD)] = jnp.concatenate(
            [result[i * HD:(i + 1) * HD] for i in range(STACK)], axis=1
        )

    def run(weighed, combined):
        hidden = hidden_of(weighed[0]) if weighed else None

        def body(step, carry):
            if combined:
                combine(combined[0], step, *combined[1])
            if weighed:
                weigh(weighed[0], hidden, step, *weighed[1])
            return carry

        lax.fori_loop(0, steps, body, 0)

    own, even, odd = (exps_own, dens_own), (exps_even, dens_even), (exps_odd, dens_odd)
    run((0, own), None)
    for t in (1, 2, 3):
        l_arrival(t).wait_recv()
        q_arrival(t).wait_recv()
    run((2, even), None)
    for j in range(4):
        kv_arrival(*value_part, 0, j).wait_recv()
        kv_arrival(*value_part, 2, j).wait_recv()
    run((1, odd), (2, even))
    o_copy(2).start()
    run((3, even), (1, odd))
    o_copy(1).start()
    run(None, (3, even))
    o_copy(3).start()
    run(None, (0, own))
    out_ref[:, columns_of(member)] = out_parts[0]

    def sent(k, carry):
        for kind in range(3):
            w_copy(kind, k).wait_send()
            c_copy(kind, k).wait_send()
        return carry

    lax.fori_loop(0, PIECES, sent, 0)
    for j in range(4):
        s_copy(j).wait_send()
        for kind in range(3):
            kv_copy(*key_part, kind, j).wait_send()
            kv_copy(*value_part, kind, j).wait_send()
    for t in (1, 2, 3):
        l_copy(t).wait_send()
        q_copy(t).wait_send()
        o_copy(t).wait_send()
        o_arrival(t).wait_recv()


def fused_local(vision, kept_index, w_key, w_value, queries, last_frame, attn_gate):
    patches, features = vision.shape[1:]
    rows, row_width = queries.shape
    width = row_width // 4
    depth = features // PIECES
    steps = width // (STACK * HD)
    vmem = pltpu.VMEM
    dma = pltpu.SemaphoreType.DMA
    exps = vmem((steps, STACK * HD, 16 * HD), jnp.bfloat16)
    dens = vmem((steps, STACK * HD, HD), jnp.float32)
    return pl.pallas_call(
        fused_kernel,
        out_shape=jax.ShapeDtypeStruct(queries.shape, jnp.bfloat16),
        in_specs=[pl.BlockSpec(memory_space=pltpu.HBM)] * 6 + [pl.BlockSpec(memory_space=pltpu.SMEM)],
        out_specs=pl.BlockSpec(memory_space=vmem),
        scratch_shapes=[
            vmem((2, patches, depth), jnp.bfloat16),
            vmem((1, HD), jnp.int32),
            vmem((1, rows), jnp.int32),
            vmem((HD, patches), jnp.bfloat16),
            vmem((PIECES, 4, HD, depth), jnp.bfloat16),
            vmem((PIECES, 2, 2, HD, depth), jnp.bfloat16),
            vmem((2, 4, HD, 2 * HD), jnp.float32),
            vmem((4, HD, 2 * HD), jnp.float32),
            vmem((16, HD, HD), jnp.bfloat16),
            vmem((16, HD, HD), jnp.bfloat16),
            vmem((4, rows, width), jnp.bfloat16),
            vmem((4, 8, HD), jnp.int32),
            exps, exps, exps, dens, dens, dens,
            vmem((4, rows, width), jnp.bfloat16),
            dma((2,)), dma((3,)), dma((2, PIECES)),
            dma((3, PIECES)), dma((3, PIECES)),
            dma((3, PIECES)), dma((3, PIECES)),
            dma((4,)), dma((4,)), dma((4,)), dma((4,)), dma((4,)), dma((4,)),
            dma((3, 4)), dma((3, 4)), dma((3, 4)), dma((3, 4)),
            dma((4,)), dma((4,)),
        ],
        compiler_params=pltpu.CompilerParams(
            collective_id=0, has_side_effects=True, vmem_limit_bytes=46 * 2**20
        ),
    )(vision, kept_index, w_key.T, w_value.T, queries, last_frame.reshape(1, rows), attn_gate)


def fold_frames(running, query_heads, last_rows, key_piece, value_piece):
    row_max, denominator, numerator = running
    frames_here = key_piece.shape[0]
    scores = jnp.einsum(
        "rkgd,fjkd->rkgfj", query_heads, key_piece, preferred_element_type=jnp.float32
    ) * HD ** (-0.5)
    frame_ids = jnp.arange(frames_here, dtype=jnp.int32)
    visible = frame_ids[None, :] <= last_rows[:, None]
    scores = jnp.where(visible[:, None, None, :, None], scores, jnp.float32(-1e30))
    new_max = jnp.maximum(row_max, jnp.max(scores, axis=(3, 4)))
    exps = jnp.exp(scores - new_max[..., None, None])
    new_denominator = jnp.sum(exps, axis=(3, 4))
    weights = exps.astype(jnp.bfloat16)
    added = jnp.einsum("rkgfj,fjkd->rkgd", weights, value_piece, preferred_element_type=jnp.float32)
    return (new_max, new_denominator, added)


def attend(rows_q, rows_last, groups, key_rows, value_rows, attn_gate):
    total_rows, row_width = rows_q.shape
    local_kv = key_rows.shape[2] // HD
    group_size = row_width // HD // local_kv
    group_rows = total_rows // groups
    query_groups = [rows_q.reshape(group_rows, local_kv, group_size, HD)]
    last_groups = [rows_last]
    initial = tuple(
        (
            (
                jnp.full((group_rows, local_kv, group_size), -1e30, jnp.float32),
                jnp.zeros((group_rows, local_kv, group_size), jnp.float32),
                jnp.zeros((group_rows, local_kv, group_size, HD), jnp.float32),
            )
            for member in range(groups)
        )
    )
    key_piece = lax.all_gather(key_rows, "blk", axis=0, tiled=True)
    value_piece = lax.all_gather(value_rows, "blk", axis=0, tiled=True)
    frames_here = key_piece.shape[0]
    key_piece = key_piece.reshape(frames_here, key_piece.shape[1], local_kv, HD)
    value_piece = value_piece.reshape(frames_here, value_piece.shape[1], local_kv, HD)
    member = 0
    query_heads = query_groups[member]
    last_rows = last_groups[member]
    state_new = fold_frames(initial[member], query_heads, last_rows, key_piece, value_piece)
    updated = [state_new]
    results = tuple(updated)
    gate_factor = jnp.tanh(attn_gate[0])
    pieces_out = [
        (gate_factor * (numerator / denominator[..., None])).reshape(group_rows, row_width)
        for row_max, denominator, numerator in results
    ]
    return pieces_out[0].astype(jnp.bfloat16)


def local(vision, kept_index, w_key, w_value, queries, last_frame, attn_gate):
    chosen = vision[0][kept_index[0]]
    stacked = jnp.stack([w_key, w_value])
    partial_value = jnp.einsum(
        "td,sdc->stc",
        chosen,
        lax.all_gather(stacked, "blk", axis=2, tiled=True),
        preferred_element_type=jnp.float32,
    )
    summed = lax.psum_scatter(partial_value, "head", scatter_dimension=2, tiled=True).astype(
        jnp.bfloat16
    )
    key_rows = summed[0][None]
    value_rows = summed[1][None]
    return attend(queries, last_frame, 1, key_rows, value_rows, attn_gate)


def solution(mesh):
    in_specs = (
        P("blk", None, "head"),
        P("blk", None),
        P("head", "blk"),
        P("head", "blk"),
        P("blk", "head"),
        P("blk"),
        P(),
    )
    out_specs = P("blk", "head")
    if dict(mesh.shape) == {"blk": 16, "head": 2}:
        return jax.shard_map(
            fused_local, mesh=mesh, in_specs=in_specs, out_specs=out_specs, check_vma=False
        )
    return jax.shard_map(local, mesh=mesh, in_specs=in_specs, out_specs=out_specs, check_vma=False)
```

```python
import jax
import jax.numpy as jnp
from jax import lax
from jax.experimental import pallas as pl
from jax.experimental.pallas import tpu as pltpu
from jax.sharding import PartitionSpec as P

HD = 128
MESH = pl.DeviceIdType.MESH
PIECES = 16
RELAY_LAG = 3
LAG = 5
STACK = 2


def fused_kernel(
    vision_ref, index_hbm, w_key_ref, w_value_ref, q_ref, last_hbm, gate_ref, out_ref,
    vision_buf, index_ref, last_ref, onehot, chosen, weights, sums, partner_sums, keys_all,
    values_all, q_all, last_all, exps_own, exps_even, exps_odd, dens_own, dens_even, dens_odd,
    out_parts, vision_sem, small_sem, load_sem,
    w_send, w_recv, c_send, c_recv, q_send, q_recv, l_send, l_recv,
    s_send, s_recv, k_send, k_recv, v_send, v_recv, o_send, o_recv,
):
    blk = lax.axis_index("blk")
    side = lax.axis_index("head")
    z1, member, x = blk // 8, (blk % 8) // 2, blk % 2
    z0, y = member // 2, member % 2
    frame_at = lambda zz, mm, xx: zz * 8 + mm * 2 + xx
    to_x = (frame_at(z1, member, 1 - x), side)
    to_z1 = (frame_at(1 - z1, member, x), side)
    to_y = (frame_at(z1, z0 * 2 + 1 - y, x), side)
    to_z0 = (frame_at(z1, (1 - z0) * 2 + y, x), side)
    to_diagonal = (frame_at(z1, (1 - z0) * 2 + 1 - y, x), side)
    to_core = (blk, 1 - side)
    partners = (to_x, to_z1, to_y, to_z0, to_diagonal, to_core)

    def send(src, dst, send_sem, recv_sem, device):
        return pltpu.make_async_remote_copy(
            src_ref=src, dst_ref=dst, send_sem=send_sem, recv_sem=recv_sem,
            device_id=device, device_id_type=MESH,
        )

    depth = chosen.shape[3]
    patches = vision_buf.shape[1]

    def vision_copy(k):
        columns = pl.ds(pl.multiple_of(k * depth, depth), depth)
        slot = lax.rem(k, 2)
        return pltpu.make_async_copy(
            vision_ref.at[0, :, columns], vision_buf.at[slot], vision_sem.at[slot]
        )

    def w_copy(kind, k):
        slot = weights.at[k, z1 if kind < 2 else 1 - z1, x]
        return send(slot, slot, w_send.at[kind, k], w_recv.at[kind, k], to_z1 if kind == 1 else to_x)

    def w_arrival(kind, k):
        slot = weights.at[k, z1 if kind == 0 else 1 - z1, x if kind == 1 else 1 - x]
        return send(slot, slot, w_send.at[kind, k], w_recv.at[kind, k], to_x)

    def c_copy(kind, k):
        slot = chosen.at[k, member if kind < 2 else (1 - z0) * 2 + y]
        return send(slot, slot, c_send.at[kind, k], c_recv.at[kind, k], to_z0 if kind == 1 else to_y)

    def c_arrival(kind, k):
        from_z0 = z0 if kind == 0 else 1 - z0
        from_y = y if kind == 1 else 1 - y
        slot = chosen.at[k, from_z0 * 2 + from_y]
        return send(slot, slot, c_send.at[kind, k], c_recv.at[kind, k], to_y)

    def kv_copy(held, send_sem, recv_sem, kind, j):
        slot = held.at[frame_at(z1 if kind < 2 else 1 - z1, j, x)]
        return send(slot, slot, send_sem.at[kind, j], recv_sem.at[kind, j], to_z1 if kind == 1 else to_x)

    def kv_arrival(held, send_sem, recv_sem, kind, j):
        slot = held.at[frame_at(z1 if kind == 0 else 1 - z1, j, x if kind == 1 else 1 - x)]
        return send(slot, slot, send_sem.at[kind, j], recv_sem.at[kind, j], to_x)

    key_part = (keys_all, k_send, k_recv)
    value_part = (values_all, v_send, v_recv)

    width = q_all.shape[2]

    def peer(t):
        return lax.rem(member + t, 4)

    def columns_of(m):
        return pl.ds(pl.multiple_of(m * width, width), width)

    def q_copy(t):
        target = (frame_at(z1, peer(t), x), side)
        return send(q_ref.at[:, columns_of(peer(t))], q_all.at[member], q_send.at[t], q_recv.at[t], target)

    def q_arrival(t):
        slot = q_all.at[peer(4 - t)]
        return send(slot, slot, q_send.at[t], q_recv.at[t], to_y)

    def l_copy(t):
        target = (frame_at(z1, peer(t), x), side)
        return send(last_all.at[member], last_all.at[member], l_send.at[t], l_recv.at[t], target)

    def l_arrival(t):
        slot = last_all.at[peer(4 - t)]
        return send(slot, slot, l_send.at[t], l_recv.at[t], to_y)

    def o_copy(t):
        target = (frame_at(z1, peer(t), x), side)
        return send(out_parts.at[t], out_ref.at[:, columns_of(member)], o_send.at[t], o_recv.at[t], target)

    def o_arrival(t):
        slot = out_ref.at[:, columns_of(peer(4 - t))]
        return send(slot, slot, o_send.at[t], o_recv.at[t], to_y)

    def s_copy(j):
        return send(sums.at[1 - side, j], partner_sums.at[j], s_send.at[j], s_recv.at[j], to_core)

    def w_load(which, k):
        columns = pl.ds(pl.multiple_of(k * depth, depth), depth)
        return pltpu.make_async_copy(
            (w_key_ref, w_value_ref)[which].at[:, columns],
            weights.at[k, z1, x, pl.ds(which * 64, 64)], load_sem.at[which, k],
        )

    own_q = pltpu.make_async_copy(q_ref.at[:, columns_of(member)], q_all.at[member], small_sem.at[0])
    index_copy = pltpu.make_async_copy(index_hbm, index_ref, small_sem.at[1])
    last_copy = pltpu.make_async_copy(last_hbm, last_ref, small_sem.at[2])

    barrier = pltpu.get_barrier_semaphore()
    for device in partners:
        pl.semaphore_signal(barrier, inc=1, device_id=device, device_id_type=MESH)

    def load_weights(k, carry):
        w_load(0, k).start()
        w_load(1, k).start()
        return carry

    index_copy.start()
    last_copy.start()
    lax.fori_loop(0, PIECES, load_weights, 0)
    vision_copy(0).start()
    vision_copy(1).start()
    own_q.start()
    pl.semaphore_wait(barrier, len(partners))

    def send_weights(k):
        w_load(0, k).wait()
        w_load(1, k).wait()
        w_copy(1, k).start()
        w_copy(0, k).start()

    send_weights(0)
    send_weights(1)
    index_copy.wait()
    last_copy.wait()
    index_rows = jnp.broadcast_to(index_ref[...], (HD, HD)).T
    lanes = lax.broadcasted_iota(jnp.int32, (HD, HD), 1)
    for start in range(0, patches, HD):
        stop = min(start + HD, patches)
        onehot[:, start:stop] = jnp.where(index_rows == lanes + start, 1.0, 0.0).astype(
            jnp.bfloat16
        )[:, :stop - start]

    def choose(k):
        vision_copy(k).wait()
        picked = jnp.dot(
            onehot[...], vision_buf[lax.rem(k, 2)], preferred_element_type=jnp.float32
        )
        chosen[k, member] = picked.astype(jnp.bfloat16)
        c_copy(1, k).start()
        c_copy(0, k).start()

    last_all[member] = jnp.broadcast_to(last_ref[...], (8, HD))
    sums[...] = jnp.zeros_like(sums)

    def project(k):
        for kind in (0, 2):
            w_arrival(kind, k).wait_recv()
            c_arrival(kind, k).wait_recv()
        rows = chosen[k].reshape(4 * HD, depth)
        for group in range(2):
            columns = weights[k, group].reshape(2 * HD, depth)
            added = lax.dot_general(
                rows, columns, (((1,), (1,)), ((), ())), preferred_element_type=jnp.float32
            )
            sums[group] += added.reshape(4, HD, 2 * HD)

    def relay(k):
        w_arrival(1, k).wait_recv()
        w_copy(2, k).start()
        c_arrival(1, k).wait_recv()
        c_copy(2, k).start()

    def step_of(k, carry):
        @pl.when(k < PIECES)
        def _():
            choose(k)

        @pl.when(k + 2 < PIECES)
        def _():
            vision_copy(k + 2).start()
            send_weights(k + 2)

        @pl.when((k >= RELAY_LAG) & (k < PIECES + RELAY_LAG))
        def _():
            relay(k - RELAY_LAG)

        @pl.when(k == PIECES + RELAY_LAG - 1)
        def _():
            for t in (1, 2, 3):
                l_copy(t).start()
                q_copy(t).start()

        @pl.when(k >= LAG)
        def _():
            project(k - LAG)

        return carry

    lax.fori_loop(0, PIECES + LAG, step_of, 0)

    for j in range(4):
        s_copy(j).start()
    for j in range(4):
        s_copy(j).wait_recv()
        total = sums[side, j] + partner_sums[j]
        key_rows = jnp.concatenate([total[:, :64], total[:, 128:192]], axis=1)
        value_rows = jnp.concatenate([total[:, 64:128], total[:, 192:]], axis=1)
        frame = frame_at(z1, j, x)
        keys_all[frame] = key_rows.T.astype(jnp.bfloat16)
        values_all[frame] = value_rows.astype(jnp.bfloat16)
        kv_copy(*key_part, 1, j).start()
        kv_copy(*key_part, 0, j).start()
    for j in range(4):
        kv_copy(*value_part, 1, j).start()
    for j in range(4):
        kv_arrival(*key_part, 1, j).wait_recv()
        kv_copy(*key_part, 2, j).start()
    for j in range(4):
        kv_copy(*value_part, 0, j).start()
    for j in range(4):
        kv_arrival(*value_part, 1, j).wait_recv()
        kv_copy(*value_part, 2, j).start()
    own_q.wait()
    for j in range(4):
        kv_arrival(*key_part, 0, j).wait_recv()
        kv_arrival(*key_part, 2, j).wait_recv()

    frames = keys_all.shape[0]
    keys = frames * HD
    gate = jnp.tanh(jnp.full((1, HD), gate_ref[0], jnp.float32))
    factor = HD ** (-0.5) * 1.4426950408889634
    steps = width // (STACK * HD)
    feature = lax.broadcasted_iota(jnp.int32, (HD, HD), 0)

    def hidden_of(t):
        last_rows = jnp.broadcast_to(last_all[peer(t), 0:1, :], (HD, HD)).T
        hidden = jnp.where(last_rows < lanes, -1e30, 0.0).astype(jnp.bfloat16)
        return jnp.concatenate([hidden] * STACK, axis=0)

    def weigh(t, hidden, step, exps_ref, dens_ref):
        start = pl.multiple_of(step * STACK * HD, STACK * HD)
        heads = q_all[peer(t), :, pl.ds(start, STACK * HD)]
        stacked = jnp.concatenate([heads[:, i * HD:(i + 1) * HD] for i in range(STACK)], axis=0)
        key_columns = jnp.concatenate([keys_all[frame] for frame in range(frames)], axis=1)
        marks = jnp.concatenate(
            [jnp.where(feature == frame, 1.0, 0.0).astype(jnp.bfloat16) for frame in range(frames)],
            axis=1,
        )
        scores = jnp.dot(
            jnp.concatenate([stacked, hidden], axis=1),
            jnp.concatenate([key_columns, marks], axis=0),
            preferred_element_type=jnp.float32,
        )
        row_max = jnp.max(scores, axis=1, keepdims=True)
        exps = jnp.exp2((scores - row_max) * factor)
        dens_ref[step] = jnp.broadcast_to(jnp.sum(exps, axis=1, keepdims=True), (STACK * HD, HD))
        exps_ref[step] = exps.astype(jnp.bfloat16)

    def combine(t, step, exps_ref, dens_ref):
        start = pl.multiple_of(step * STACK * HD, STACK * HD)
        value_rows = values_all[...].reshape(keys, HD)
        numerator = jnp.dot(exps_ref[step], value_rows, preferred_element_type=jnp.float32)
        result = (gate * (numerator / dens_ref[step])).astype(jnp.bfloat16)
        out_parts[t, :, pl.ds(start, STACK * HD)] = jnp.concatenate(
            [result[i * HD:(i + 1) * HD] for i in range(STACK)], axis=1
        )

    def run(weighed, combined):
        hidden = hidden_of(weighed[0]) if weighed else None

        def body(step, carry):
            if combined:
                combine(combined[0], step, *combined[1])
            if weighed:
                weigh(weighed[0], hidden, step, *weighed[1])
            return carry

        lax.fori_loop(0, steps, body, 0)

    own, even, odd = (exps_own, dens_own), (exps_even, dens_even), (exps_odd, dens_odd)
    run((0, own), None)
    for t in (1, 2, 3):
        l_arrival(t).wait_recv()
        q_arrival(t).wait_recv()
    run((2, even), None)
    for j in range(4):
        kv_arrival(*value_part, 0, j).wait_recv()
        kv_arrival(*value_part, 2, j).wait_recv()
    run((1, odd), (2, even))
    o_copy(2).start()
    run((3, even), (1, odd))
    o_copy(1).start()
    run(None, (3, even))
    o_copy(3).start()
    run(None, (0, own))
    out_ref[:, columns_of(member)] = out_parts[0]

    def sent(k, carry):
        for kind in range(3):
            w_copy(kind, k).wait_send()
            c_copy(kind, k).wait_send()
        return carry

    lax.fori_loop(0, PIECES, sent, 0)
    for j in range(4):
        s_copy(j).wait_send()
        for kind in range(3):
            kv_copy(*key_part, kind, j).wait_send()
            kv_copy(*value_part, kind, j).wait_send()
    for t in (1, 2, 3):
        l_copy(t).wait_send()
        q_copy(t).wait_send()
        o_copy(t).wait_send()
        o_arrival(t).wait_recv()


def fused_local(vision, kept_index, w_key, w_value, queries, last_frame, attn_gate):
    patches, features = vision.shape[1:]
    rows, row_width = queries.shape
    width = row_width // 4
    depth = features // PIECES
    steps = width // (STACK * HD)
    vmem = pltpu.VMEM
    dma = pltpu.SemaphoreType.DMA
    exps = vmem((steps, STACK * HD, 16 * HD), jnp.bfloat16)
    dens = vmem((steps, STACK * HD, HD), jnp.float32)
    return pl.pallas_call(
        fused_kernel,
        out_shape=jax.ShapeDtypeStruct(queries.shape, jnp.bfloat16),
        in_specs=[pl.BlockSpec(memory_space=pltpu.HBM)] * 6 + [pl.BlockSpec(memory_space=pltpu.SMEM)],
        out_specs=pl.BlockSpec(memory_space=vmem),
        scratch_shapes=[
            vmem((2, patches, depth), jnp.bfloat16),
            vmem((1, HD), jnp.int32),
            vmem((1, rows), jnp.int32),
            vmem((HD, patches), jnp.bfloat16),
            vmem((PIECES, 4, HD, depth), jnp.bfloat16),
            vmem((PIECES, 2, 2, HD, depth), jnp.bfloat16),
            vmem((2, 4, HD, 2 * HD), jnp.float32),
            vmem((4, HD, 2 * HD), jnp.float32),
            vmem((16, HD, HD), jnp.bfloat16),
            vmem((16, HD, HD), jnp.bfloat16),
            vmem((4, rows, width), jnp.bfloat16),
            vmem((4, 8, HD), jnp.int32),
            exps, exps, exps, dens, dens, dens,
            vmem((4, rows, width), jnp.bfloat16),
            dma((2,)), dma((3,)), dma((2, PIECES)),
            dma((3, PIECES)), dma((3, PIECES)),
            dma((3, PIECES)), dma((3, PIECES)),
            dma((4,)), dma((4,)), dma((4,)), dma((4,)), dma((4,)), dma((4,)),
            dma((3, 4)), dma((3, 4)), dma((3, 4)), dma((3, 4)),
            dma((4,)), dma((4,)),
        ],
        compiler_params=pltpu.CompilerParams(
            collective_id=0, has_side_effects=True, vmem_limit_bytes=56 * 2**20
        ),
    )(vision, kept_index, w_key.T, w_value.T, queries, last_frame.reshape(1, rows), attn_gate)


def fold_frames(running, query_heads, last_rows, key_piece, value_piece):
    row_max, denominator, numerator = running
    frames_here = key_piece.shape[0]
    scores = jnp.einsum(
        "rkgd,fjkd->rkgfj", query_heads, key_piece, preferred_element_type=jnp.float32
    ) * HD ** (-0.5)
    frame_ids = jnp.arange(frames_here, dtype=jnp.int32)
    visible = frame_ids[None, :] <= last_rows[:, None]
    scores = jnp.where(visible[:, None, None, :, None], scores, jnp.float32(-1e30))
    new_max = jnp.maximum(row_max, jnp.max(scores, axis=(3, 4)))
    exps = jnp.exp(scores - new_max[..., None, None])
    new_denominator = jnp.sum(exps, axis=(3, 4))
    weights = exps.astype(jnp.bfloat16)
    added = jnp.einsum("rkgfj,fjkd->rkgd", weights, value_piece, preferred_element_type=jnp.float32)
    return (new_max, new_denominator, added)


def attend(rows_q, rows_last, groups, key_rows, value_rows, attn_gate):
    total_rows, row_width = rows_q.shape
    local_kv = key_rows.shape[2] // HD
    group_size = row_width // HD // local_kv
    group_rows = total_rows // groups
    query_groups = [rows_q.reshape(group_rows, local_kv, group_size, HD)]
    last_groups = [rows_last]
    initial = tuple(
        (
            (
                jnp.full((group_rows, local_kv, group_size), -1e30, jnp.float32),
                jnp.zeros((group_rows, local_kv, group_size), jnp.float32),
                jnp.zeros((group_rows, local_kv, group_size, HD), jnp.float32),
            )
            for member in range(groups)
        )
    )
    key_piece = lax.all_gather(key_rows, "blk", axis=0, tiled=True)
    value_piece = lax.all_gather(value_rows, "blk", axis=0, tiled=True)
    frames_here = key_piece.shape[0]
    key_piece = key_piece.reshape(frames_here, key_piece.shape[1], local_kv, HD)
    value_piece = value_piece.reshape(frames_here, value_piece.shape[1], local_kv, HD)
    member = 0
    query_heads = query_groups[member]
    last_rows = last_groups[member]
    state_new = fold_frames(initial[member], query_heads, last_rows, key_piece, value_piece)
    updated = [state_new]
    results = tuple(updated)
    gate_factor = jnp.tanh(attn_gate[0])
    pieces_out = [
        (gate_factor * (numerator / denominator[..., None])).reshape(group_rows, row_width)
        for row_max, denominator, numerator in results
    ]
    return pieces_out[0].astype(jnp.bfloat16)


def local(vision, kept_index, w_key, w_value, queries, last_frame, attn_gate):
    chosen = vision[0][kept_index[0]]
    stacked = jnp.stack([w_key, w_value])
    partial_value = jnp.einsum(
        "td,sdc->stc",
        chosen,
        lax.all_gather(stacked, "blk", axis=2, tiled=True),
        preferred_element_type=jnp.float32,
    )
    summed = lax.psum_scatter(partial_value, "head", scatter_dimension=2, tiled=True).astype(
        jnp.bfloat16
    )
    key_rows = summed[0][None]
    value_rows = summed[1][None]
    return attend(queries, last_frame, 1, key_rows, value_rows, attn_gate)


def solution(mesh):
    in_specs = (
        P("blk", None, "head"),
        P("blk", None),
        P("head", "blk"),
        P("head", "blk"),
        P("blk", "head"),
        P("blk"),
        P(),
    )
    out_specs = P("blk", "head")
    if dict(mesh.shape) == {"blk": 16, "head": 2}:
        return jax.shard_map(
            fused_local, mesh=mesh, in_specs=in_specs, out_specs=out_specs, check_vma=False
        )
    return jax.shard_map(local, mesh=mesh, in_specs=in_specs, out_specs=out_specs, check_vma=False)
```

```python
import jax
import jax.numpy as jnp
from jax import lax
from jax.experimental import pallas as pl
from jax.experimental.pallas import tpu as pltpu
from jax.sharding import PartitionSpec as P

HD = 128
MESH = pl.DeviceIdType.MESH
PIECES = 16
RELAY_LAG = 3
LAG = 5
STACK = 4


def fused_kernel(
    vision_ref, index_hbm, w_key_ref, w_value_ref, q_ref, last_hbm, gate_ref, out_ref,
    vision_buf, index_ref, last_ref, onehot, chosen, weights, sums, partner_sums, keys_all,
    values_all, q_all, last_all, exps_own, exps_even, exps_odd, dens_own, dens_even, dens_odd,
    out_parts, vision_sem, small_sem, load_sem,
    w_send, w_recv, c_send, c_recv, q_send, q_recv, l_send, l_recv,
    s_send, s_recv, k_send, k_recv, v_send, v_recv, o_send, o_recv,
):
    blk = lax.axis_index("blk")
    side = lax.axis_index("head")
    z1, member, x = blk // 8, (blk % 8) // 2, blk % 2
    z0, y = member // 2, member % 2
    frame_at = lambda zz, mm, xx: zz * 8 + mm * 2 + xx
    to_x = (frame_at(z1, member, 1 - x), side)
    to_z1 = (frame_at(1 - z1, member, x), side)
    to_y = (frame_at(z1, z0 * 2 + 1 - y, x), side)
    to_z0 = (frame_at(z1, (1 - z0) * 2 + y, x), side)
    to_diagonal = (frame_at(z1, (1 - z0) * 2 + 1 - y, x), side)
    to_core = (blk, 1 - side)
    partners = (to_x, to_z1, to_y, to_z0, to_diagonal, to_core)

    def send(src, dst, send_sem, recv_sem, device):
        return pltpu.make_async_remote_copy(
            src_ref=src, dst_ref=dst, send_sem=send_sem, recv_sem=recv_sem,
            device_id=device, device_id_type=MESH,
        )

    depth = chosen.shape[3]
    patches = vision_buf.shape[1]

    def vision_copy(k):
        columns = pl.ds(pl.multiple_of(k * depth, depth), depth)
        slot = lax.rem(k, 2)
        return pltpu.make_async_copy(
            vision_ref.at[0, :, columns], vision_buf.at[slot], vision_sem.at[slot]
        )

    def w_copy(kind, k):
        slot = weights.at[k, z1 if kind < 2 else 1 - z1, x]
        return send(slot, slot, w_send.at[kind, k], w_recv.at[kind, k], to_z1 if kind == 1 else to_x)

    def w_arrival(kind, k):
        slot = weights.at[k, z1 if kind == 0 else 1 - z1, x if kind == 1 else 1 - x]
        return send(slot, slot, w_send.at[kind, k], w_recv.at[kind, k], to_x)

    def c_copy(kind, k):
        slot = chosen.at[k, member if kind < 2 else (1 - z0) * 2 + y]
        return send(slot, slot, c_send.at[kind, k], c_recv.at[kind, k], to_z0 if kind == 1 else to_y)

    def c_arrival(kind, k):
        from_z0 = z0 if kind == 0 else 1 - z0
        from_y = y if kind == 1 else 1 - y
        slot = chosen.at[k, from_z0 * 2 + from_y]
        return send(slot, slot, c_send.at[kind, k], c_recv.at[kind, k], to_y)

    def kv_copy(held, send_sem, recv_sem, kind, j):
        slot = held.at[frame_at(z1 if kind < 2 else 1 - z1, j, x), pl.ds(0, HD)]
        return send(slot, slot, send_sem.at[kind, j], recv_sem.at[kind, j], to_z1 if kind == 1 else to_x)

    def kv_arrival(held, send_sem, recv_sem, kind, j):
        frame = frame_at(z1 if kind == 0 else 1 - z1, j, x if kind == 1 else 1 - x)
        slot = held.at[frame, pl.ds(0, HD)]
        return send(slot, slot, send_sem.at[kind, j], recv_sem.at[kind, j], to_x)

    key_part = (keys_all, k_send, k_recv)
    value_part = (values_all, v_send, v_recv)

    width = q_all.shape[2]

    def peer(t):
        return lax.rem(member + t, 4)

    def columns_of(m):
        return pl.ds(pl.multiple_of(m * width, width), width)

    def q_copy(t):
        target = (frame_at(z1, peer(t), x), side)
        return send(q_ref.at[:, columns_of(peer(t))], q_all.at[member], q_send.at[t], q_recv.at[t], target)

    def q_arrival(t):
        slot = q_all.at[peer(4 - t)]
        return send(slot, slot, q_send.at[t], q_recv.at[t], to_y)

    def l_copy(t):
        target = (frame_at(z1, peer(t), x), side)
        return send(last_all.at[member], last_all.at[member], l_send.at[t], l_recv.at[t], target)

    def l_arrival(t):
        slot = last_all.at[peer(4 - t)]
        return send(slot, slot, l_send.at[t], l_recv.at[t], to_y)

    def o_copy(t):
        target = (frame_at(z1, peer(t), x), side)
        return send(out_parts.at[t], out_ref.at[:, columns_of(member)], o_send.at[t], o_recv.at[t], target)

    def o_arrival(t):
        slot = out_ref.at[:, columns_of(peer(4 - t))]
        return send(slot, slot, o_send.at[t], o_recv.at[t], to_y)

    def s_copy(j):
        return send(sums.at[1 - side, j], partner_sums.at[j], s_send.at[j], s_recv.at[j], to_core)

    def w_load(which, k):
        columns = pl.ds(pl.multiple_of(k * depth, depth), depth)
        return pltpu.make_async_copy(
            (w_key_ref, w_value_ref)[which].at[:, columns],
            weights.at[k, z1, x, pl.ds(which * 64, 64)], load_sem.at[which, k],
        )

    own_q = pltpu.make_async_copy(q_ref.at[:, columns_of(member)], q_all.at[member], small_sem.at[0])
    index_copy = pltpu.make_async_copy(index_hbm, index_ref, small_sem.at[1])
    last_copy = pltpu.make_async_copy(last_hbm, last_ref, small_sem.at[2])

    barrier = pltpu.get_barrier_semaphore()
    for device in partners:
        pl.semaphore_signal(barrier, inc=1, device_id=device, device_id_type=MESH)

    def load_weights(k, carry):
        w_load(0, k).start()
        w_load(1, k).start()
        return carry

    index_copy.start()
    last_copy.start()
    lax.fori_loop(0, PIECES, load_weights, 0)
    vision_copy(0).start()
    vision_copy(1).start()
    own_q.start()
    pl.semaphore_wait(barrier, len(partners))

    def send_weights(k):
        w_load(0, k).wait()
        w_load(1, k).wait()
        w_copy(1, k).start()
        w_copy(0, k).start()

    send_weights(0)
    send_weights(1)
    index_copy.wait()
    last_copy.wait()
    index_rows = jnp.broadcast_to(index_ref[...], (HD, HD)).T
    lanes = lax.broadcasted_iota(jnp.int32, (HD, HD), 1)
    for start in range(0, patches, HD):
        stop = min(start + HD, patches)
        onehot[:, start:stop] = jnp.where(index_rows == lanes + start, 1.0, 0.0).astype(
            jnp.bfloat16
        )[:, :stop - start]

    def choose(k):
        vision_copy(k).wait()
        picked = jnp.dot(
            onehot[...], vision_buf[lax.rem(k, 2)], preferred_element_type=jnp.float32
        )
        chosen[k, member] = picked.astype(jnp.bfloat16)
        c_copy(1, k).start()
        c_copy(0, k).start()

    last_all[member] = jnp.broadcast_to(last_ref[...], (8, HD))
    sums[...] = jnp.zeros_like(sums)
    feature = lax.broadcasted_iota(jnp.int32, (HD, HD), 0)
    for frame in range(keys_all.shape[0]):
        keys_all[frame, HD:] = jnp.where(feature == frame, 1.0, 0.0).astype(jnp.bfloat16)

    def project(k):
        for kind in (0, 2):
            w_arrival(kind, k).wait_recv()
            c_arrival(kind, k).wait_recv()
        rows = chosen[k].reshape(4 * HD, depth)
        for group in range(2):
            columns = weights[k, group].reshape(2 * HD, depth)
            added = lax.dot_general(
                rows, columns, (((1,), (1,)), ((), ())), preferred_element_type=jnp.float32
            )
            sums[group] += added.reshape(4, HD, 2 * HD)

    def relay(k):
        w_arrival(1, k).wait_recv()
        w_copy(2, k).start()
        c_arrival(1, k).wait_recv()
        c_copy(2, k).start()

    def step_of(k, carry):
        @pl.when(k < PIECES)
        def _():
            choose(k)

        @pl.when(k + 2 < PIECES)
        def _():
            vision_copy(k + 2).start()
            send_weights(k + 2)

        @pl.when((k >= RELAY_LAG) & (k < PIECES + RELAY_LAG))
        def _():
            relay(k - RELAY_LAG)

        @pl.when(k == PIECES + RELAY_LAG - 1)
        def _():
            for t in (1, 2, 3):
                l_copy(t).start()
                q_copy(t).start()

        @pl.when(k >= LAG)
        def _():
            project(k - LAG)

        return carry

    lax.fori_loop(0, PIECES + LAG, step_of, 0)

    for j in range(4):
        s_copy(j).start()
    for j in range(4):
        s_copy(j).wait_recv()
        total = sums[side, j] + partner_sums[j]
        key_rows = jnp.concatenate([total[:, :64], total[:, 128:192]], axis=1)
        value_rows = jnp.concatenate([total[:, 64:128], total[:, 192:]], axis=1)
        frame = frame_at(z1, j, x)
        keys_all[frame, 0:HD] = key_rows.T.astype(jnp.bfloat16)
        values_all[frame] = value_rows.astype(jnp.bfloat16)
        kv_copy(*key_part, 1, j).start()
        kv_copy(*key_part, 0, j).start()
    for j in range(4):
        kv_copy(*value_part, 1, j).start()
    for j in range(4):
        kv_arrival(*key_part, 1, j).wait_recv()
        kv_copy(*key_part, 2, j).start()
    for j in range(4):
        kv_copy(*value_part, 0, j).start()
    for j in range(4):
        kv_arrival(*value_part, 1, j).wait_recv()
        kv_copy(*value_part, 2, j).start()
    own_q.wait()
    for j in range(4):
        kv_arrival(*key_part, 0, j).wait_recv()
        kv_arrival(*key_part, 2, j).wait_recv()

    frames = keys_all.shape[0]
    keys = frames * HD
    gate = jnp.tanh(jnp.full((1, HD), gate_ref[0], jnp.float32))
    factor = HD ** (-0.5) * 1.4426950408889634
    steps = width // (STACK * HD)

    def hidden_of(t):
        last_rows = jnp.broadcast_to(last_all[peer(t), 0:1, :], (HD, HD)).T
        hidden = jnp.where(last_rows < lanes, -1e30, 0.0).astype(jnp.bfloat16)
        return jnp.concatenate([hidden] * STACK, axis=0)

    def weigh(t, hidden, step, exps_ref, dens_ref):
        start = pl.multiple_of(step * STACK * HD, STACK * HD)
        heads = q_all[peer(t), :, pl.ds(start, STACK * HD)]
        stacked = jnp.concatenate([heads[:, i * HD:(i + 1) * HD] for i in range(STACK)], axis=0)
        key_columns = jnp.concatenate([keys_all[frame] for frame in range(frames)], axis=1)
        scores = jnp.dot(
            jnp.concatenate([stacked, hidden], axis=1),
            key_columns,
            preferred_element_type=jnp.float32,
        )
        row_max = jnp.max(scores, axis=1, keepdims=True)
        exps = jnp.exp2((scores - row_max) * factor)
        dens_ref[step] = jnp.broadcast_to(jnp.sum(exps, axis=1, keepdims=True), (STACK * HD, HD))
        exps_ref[step] = exps.astype(jnp.bfloat16)

    def combine(t, step, exps_ref, dens_ref):
        start = pl.multiple_of(step * STACK * HD, STACK * HD)
        value_rows = values_all[...].reshape(keys, HD)
        numerator = jnp.dot(exps_ref[step], value_rows, preferred_element_type=jnp.float32)
        result = (gate * (numerator / dens_ref[step])).astype(jnp.bfloat16)
        out_parts[t, :, pl.ds(start, STACK * HD)] = jnp.concatenate(
            [result[i * HD:(i + 1) * HD] for i in range(STACK)], axis=1
        )

    def run(weighed, combined):
        hidden = hidden_of(weighed[0]) if weighed else None

        def body(step, carry):
            if combined:
                combine(combined[0], step, *combined[1])
            if weighed:
                weigh(weighed[0], hidden, step, *weighed[1])
            return carry

        lax.fori_loop(0, steps, body, 0)

    own, even, odd = (exps_own, dens_own), (exps_even, dens_even), (exps_odd, dens_odd)
    run((0, own), None)
    for t in (1, 2, 3):
        l_arrival(t).wait_recv()
        q_arrival(t).wait_recv()
    run((2, even), None)
    for j in range(4):
        kv_arrival(*value_part, 0, j).wait_recv()
        kv_arrival(*value_part, 2, j).wait_recv()
    run((1, odd), (2, even))
    o_copy(2).start()
    run((3, even), (1, odd))
    o_copy(1).start()
    run(None, (3, even))
    o_copy(3).start()
    run(None, (0, own))
    out_ref[:, columns_of(member)] = out_parts[0]

    def sent(k, carry):
        for kind in range(3):
            w_copy(kind, k).wait_send()
            c_copy(kind, k).wait_send()
        return carry

    lax.fori_loop(0, PIECES, sent, 0)
    for j in range(4):
        s_copy(j).wait_send()
        for kind in range(3):
            kv_copy(*key_part, kind, j).wait_send()
            kv_copy(*value_part, kind, j).wait_send()
    for t in (1, 2, 3):
        l_copy(t).wait_send()
        q_copy(t).wait_send()
        o_copy(t).wait_send()
        o_arrival(t).wait_recv()


def fused_local(vision, kept_index, w_key, w_value, queries, last_frame, attn_gate):
    patches, features = vision.shape[1:]
    rows, row_width = queries.shape
    width = row_width // 4
    depth = features // PIECES
    steps = width // (STACK * HD)
    vmem = pltpu.VMEM
    dma = pltpu.SemaphoreType.DMA
    exps = vmem((steps, STACK * HD, 16 * HD), jnp.bfloat16)
    dens = vmem((steps, STACK * HD, HD), jnp.float32)
    return pl.pallas_call(
        fused_kernel,
        out_shape=jax.ShapeDtypeStruct(queries.shape, jnp.bfloat16),
        in_specs=[pl.BlockSpec(memory_space=pltpu.HBM)] * 6 + [pl.BlockSpec(memory_space=pltpu.SMEM)],
        out_specs=pl.BlockSpec(memory_space=vmem),
        scratch_shapes=[
            vmem((2, patches, depth), jnp.bfloat16),
            vmem((1, HD), jnp.int32),
            vmem((1, rows), jnp.int32),
            vmem((HD, patches), jnp.bfloat16),
            vmem((PIECES, 4, HD, depth), jnp.bfloat16),
            vmem((PIECES, 2, 2, HD, depth), jnp.bfloat16),
            vmem((2, 4, HD, 2 * HD), jnp.float32),
            vmem((4, HD, 2 * HD), jnp.float32),
            vmem((16, 2 * HD, HD), jnp.bfloat16),
            vmem((16, HD, HD), jnp.bfloat16),
            vmem((4, rows, width), jnp.bfloat16),
            vmem((4, 8, HD), jnp.int32),
            exps, exps, exps, dens, dens, dens,
            vmem((4, rows, width), jnp.bfloat16),
            dma((2,)), dma((3,)), dma((2, PIECES)),
            dma((3, PIECES)), dma((3, PIECES)),
            dma((3, PIECES)), dma((3, PIECES)),
            dma((4,)), dma((4,)), dma((4,)), dma((4,)), dma((4,)), dma((4,)),
            dma((3, 4)), dma((3, 4)), dma((3, 4)), dma((3, 4)),
            dma((4,)), dma((4,)),
        ],
        compiler_params=pltpu.CompilerParams(
            collective_id=0, has_side_effects=True, vmem_limit_bytes=56 * 2**20
        ),
    )(vision, kept_index, w_key.T, w_value.T, queries, last_frame.reshape(1, rows), attn_gate)


def fold_frames(running, query_heads, last_rows, key_piece, value_piece):
    row_max, denominator, numerator = running
    frames_here = key_piece.shape[0]
    scores = jnp.einsum(
        "rkgd,fjkd->rkgfj", query_heads, key_piece, preferred_element_type=jnp.float32
    ) * HD ** (-0.5)
    frame_ids = jnp.arange(frames_here, dtype=jnp.int32)
    visible = frame_ids[None, :] <= last_rows[:, None]
    scores = jnp.where(visible[:, None, None, :, None], scores, jnp.float32(-1e30))
    new_max = jnp.maximum(row_max, jnp.max(scores, axis=(3, 4)))
    exps = jnp.exp(scores - new_max[..., None, None])
    new_denominator = jnp.sum(exps, axis=(3, 4))
    weights = exps.astype(jnp.bfloat16)
    added = jnp.einsum("rkgfj,fjkd->rkgd", weights, value_piece, preferred_element_type=jnp.float32)
    return (new_max, new_denominator, added)


def attend(rows_q, rows_last, groups, key_rows, value_rows, attn_gate):
    total_rows, row_width = rows_q.shape
    local_kv = key_rows.shape[2] // HD
    group_size = row_width // HD // local_kv
    group_rows = total_rows // groups
    query_groups = [rows_q.reshape(group_rows, local_kv, group_size, HD)]
    last_groups = [rows_last]
    initial = tuple(
        (
            (
                jnp.full((group_rows, local_kv, group_size), -1e30, jnp.float32),
                jnp.zeros((group_rows, local_kv, group_size), jnp.float32),
                jnp.zeros((group_rows, local_kv, group_size, HD), jnp.float32),
            )
            for member in range(groups)
        )
    )
    key_piece = lax.all_gather(key_rows, "blk", axis=0, tiled=True)
    value_piece = lax.all_gather(value_rows, "blk", axis=0, tiled=True)
    frames_here = key_piece.shape[0]
    key_piece = key_piece.reshape(frames_here, key_piece.shape[1], local_kv, HD)
    value_piece = value_piece.reshape(frames_here, value_piece.shape[1], local_kv, HD)
    member = 0
    query_heads = query_groups[member]
    last_rows = last_groups[member]
    state_new = fold_frames(initial[member], query_heads, last_rows, key_piece, value_piece)
    updated = [state_new]
    results = tuple(updated)
    gate_factor = jnp.tanh(attn_gate[0])
    pieces_out = [
        (gate_factor * (numerator / denominator[..., None])).reshape(group_rows, row_width)
        for row_max, denominator, numerator in results
    ]
    return pieces_out[0].astype(jnp.bfloat16)


def local(vision, kept_index, w_key, w_value, queries, last_frame, attn_gate):
    chosen = vision[0][kept_index[0]]
    stacked = jnp.stack([w_key, w_value])
    partial_value = jnp.einsum(
        "td,sdc->stc",
        chosen,
        lax.all_gather(stacked, "blk", axis=2, tiled=True),
        preferred_element_type=jnp.float32,
    )
    summed = lax.psum_scatter(partial_value, "head", scatter_dimension=2, tiled=True).astype(
        jnp.bfloat16
    )
    key_rows = summed[0][None]
    value_rows = summed[1][None]
    return attend(queries, last_frame, 1, key_rows, value_rows, attn_gate)


def solution(mesh):
    in_specs = (
        P("blk", None, "head"),
        P("blk", None),
        P("head", "blk"),
        P("head", "blk"),
        P("blk", "head"),
        P("blk"),
        P(),
    )
    out_specs = P("blk", "head")
    if dict(mesh.shape) == {"blk": 16, "head": 2}:
        return jax.shard_map(
            fused_local, mesh=mesh, in_specs=in_specs, out_specs=out_specs, check_vma=False
        )
    return jax.shard_map(local, mesh=mesh, in_specs=in_specs, out_specs=out_specs, check_vma=False)
```

```python
import jax
import jax.numpy as jnp
from jax import lax
from jax.experimental import pallas as pl
from jax.experimental.pallas import tpu as pltpu
from jax.sharding import PartitionSpec as P

HD = 128
MESH = pl.DeviceIdType.MESH
PIECES = 16
RELAY_LAG = 3
LAG = 5
STACK = 4


def fused_kernel(
    vision_ref, index_hbm, w_key_ref, w_value_ref, q_ref, last_hbm, gate_ref, out_ref,
    vision_buf, index_ref, last_ref, onehot, chosen, weights, sums, partner_sums, keys_all,
    values_all, q_all, last_all, exps_own, exps_even, exps_odd, dens_own, dens_even, dens_odd,
    out_parts, vision_sem, small_sem, load_sem,
    w_send, w_recv, c_send, c_recv, q_send, q_recv, l_send, l_recv,
    s_send, s_recv, k_send, k_recv, v_send, v_recv, o_send, o_recv,
):
    blk = lax.axis_index("blk")
    side = lax.axis_index("head")
    z1, member, x = blk // 8, (blk % 8) // 2, blk % 2
    z0, y = member // 2, member % 2
    frame_at = lambda zz, mm, xx: zz * 8 + mm * 2 + xx
    to_x = (frame_at(z1, member, 1 - x), side)
    to_z1 = (frame_at(1 - z1, member, x), side)
    to_y = (frame_at(z1, z0 * 2 + 1 - y, x), side)
    to_z0 = (frame_at(z1, (1 - z0) * 2 + y, x), side)
    to_diagonal = (frame_at(z1, (1 - z0) * 2 + 1 - y, x), side)
    to_core = (blk, 1 - side)
    partners = (to_x, to_z1, to_y, to_z0, to_diagonal, to_core)

    def send(src, dst, send_sem, recv_sem, device):
        return pltpu.make_async_remote_copy(
            src_ref=src, dst_ref=dst, send_sem=send_sem, recv_sem=recv_sem,
            device_id=device, device_id_type=MESH,
        )

    depth = chosen.shape[3]
    patches = vision_buf.shape[1]

    def vision_copy(k):
        columns = pl.ds(pl.multiple_of(k * depth, depth), depth)
        slot = lax.rem(k, 2)
        return pltpu.make_async_copy(
            vision_ref.at[0, :, columns], vision_buf.at[slot], vision_sem.at[slot]
        )

    def w_copy(kind, k):
        slot = weights.at[k, z1 if kind < 2 else 1 - z1, x]
        return send(slot, slot, w_send.at[kind, k], w_recv.at[kind, k], to_z1 if kind == 1 else to_x)

    def w_arrival(kind, k):
        slot = weights.at[k, z1 if kind == 0 else 1 - z1, x if kind == 1 else 1 - x]
        return send(slot, slot, w_send.at[kind, k], w_recv.at[kind, k], to_x)

    def c_copy(kind, k):
        slot = chosen.at[k, member if kind < 2 else (1 - z0) * 2 + y]
        return send(slot, slot, c_send.at[kind, k], c_recv.at[kind, k], to_z0 if kind == 1 else to_y)

    def c_arrival(kind, k):
        from_z0 = z0 if kind == 0 else 1 - z0
        from_y = y if kind == 1 else 1 - y
        slot = chosen.at[k, from_z0 * 2 + from_y]
        return send(slot, slot, c_send.at[kind, k], c_recv.at[kind, k], to_y)

    def kv_copy(held, send_sem, recv_sem, kind, j):
        slot = held.at[frame_at(z1 if kind < 2 else 1 - z1, j, x), pl.ds(0, HD)]
        return send(slot, slot, send_sem.at[kind, j], recv_sem.at[kind, j], to_z1 if kind == 1 else to_x)

    def kv_arrival(held, send_sem, recv_sem, kind, j):
        frame = frame_at(z1 if kind == 0 else 1 - z1, j, x if kind == 1 else 1 - x)
        slot = held.at[frame, pl.ds(0, HD)]
        return send(slot, slot, send_sem.at[kind, j], recv_sem.at[kind, j], to_x)

    key_part = (keys_all, k_send, k_recv)
    value_part = (values_all, v_send, v_recv)

    width = q_all.shape[2]

    def peer(t):
        return (1 - z0 if t // 2 else z0) * 2 + (1 - y if t % 2 else y)

    def columns_of(m):
        return pl.ds(pl.multiple_of(m * width, width), width)

    def q_copy(t):
        target = (frame_at(z1, peer(t), x), side)
        return send(q_ref.at[:, columns_of(peer(t))], q_all.at[member], q_send.at[t], q_recv.at[t], target)

    def q_arrival(t):
        slot = q_all.at[peer(t)]
        return send(slot, slot, q_send.at[t], q_recv.at[t], to_y)

    def l_copy(t):
        target = (frame_at(z1, peer(t), x), side)
        return send(last_all.at[member], last_all.at[member], l_send.at[t], l_recv.at[t], target)

    def l_arrival(t):
        slot = last_all.at[peer(t)]
        return send(slot, slot, l_send.at[t], l_recv.at[t], to_y)

    def o_copy(t):
        target = (frame_at(z1, peer(t), x), side)
        return send(out_parts.at[t], out_ref.at[:, columns_of(member)], o_send.at[t], o_recv.at[t], target)

    def o_arrival(t):
        slot = out_ref.at[:, columns_of(peer(t))]
        return send(slot, slot, o_send.at[t], o_recv.at[t], to_y)

    def s_copy(j):
        return send(sums.at[1 - side, j], partner_sums.at[j], s_send.at[j], s_recv.at[j], to_core)

    def w_load(which, k):
        columns = pl.ds(pl.multiple_of(k * depth, depth), depth)
        return pltpu.make_async_copy(
            (w_key_ref, w_value_ref)[which].at[:, columns],
            weights.at[k, z1, x, pl.ds(which * 64, 64)], load_sem.at[which, k],
        )

    own_q = pltpu.make_async_copy(q_ref.at[:, columns_of(member)], q_all.at[member], small_sem.at[0])
    index_copy = pltpu.make_async_copy(index_hbm, index_ref, small_sem.at[1])
    last_copy = pltpu.make_async_copy(last_hbm, last_ref, small_sem.at[2])

    barrier = pltpu.get_barrier_semaphore()
    for device in partners:
        pl.semaphore_signal(barrier, inc=1, device_id=device, device_id_type=MESH)

    def load_weights(k, carry):
        w_load(0, k).start()
        w_load(1, k).start()
        return carry

    index_copy.start()
    last_copy.start()
    lax.fori_loop(0, PIECES, load_weights, 0)
    vision_copy(0).start()
    vision_copy(1).start()
    own_q.start()
    pl.semaphore_wait(barrier, len(partners))

    def send_weights(k):
        w_load(0, k).wait()
        w_load(1, k).wait()
        w_copy(1, k).start()
        w_copy(0, k).start()

    send_weights(0)
    send_weights(1)
    index_copy.wait()
    last_copy.wait()
    index_rows = jnp.broadcast_to(index_ref[...], (HD, HD)).T
    lanes = lax.broadcasted_iota(jnp.int32, (HD, HD), 1)
    for start in range(0, patches, HD):
        stop = min(start + HD, patches)
        onehot[:, start:stop] = jnp.where(index_rows == lanes + start, 1.0, 0.0).astype(
            jnp.bfloat16
        )[:, :stop - start]

    def choose(k):
        vision_copy(k).wait()
        picked = jnp.dot(
            onehot[...], vision_buf[lax.rem(k, 2)], preferred_element_type=jnp.float32
        )
        chosen[k, member] = picked.astype(jnp.bfloat16)
        c_copy(1, k).start()
        c_copy(0, k).start()

    last_all[member] = jnp.broadcast_to(last_ref[...], (8, HD))
    sums[...] = jnp.zeros_like(sums)
    feature = lax.broadcasted_iota(jnp.int32, (HD, HD), 0)
    for frame in range(keys_all.shape[0]):
        keys_all[frame, HD:] = jnp.where(feature == frame, 1.0, 0.0).astype(jnp.bfloat16)

    def project(k):
        for kind in (0, 2):
            w_arrival(kind, k).wait_recv()
            c_arrival(kind, k).wait_recv()
        rows = chosen[k].reshape(4 * HD, depth)
        for group in range(2):
            columns = weights[k, group].reshape(2 * HD, depth)
            added = lax.dot_general(
                rows, columns, (((1,), (1,)), ((), ())), preferred_element_type=jnp.float32
            )
            sums[group] += added.reshape(4, HD, 2 * HD)

    def relay(k):
        w_arrival(1, k).wait_recv()
        w_copy(2, k).start()
        c_arrival(1, k).wait_recv()
        c_copy(2, k).start()

    def step_of(k, carry):
        @pl.when(k < PIECES)
        def _():
            choose(k)

        @pl.when(k + 2 < PIECES)
        def _():
            vision_copy(k + 2).start()
            send_weights(k + 2)

        @pl.when((k >= RELAY_LAG) & (k < PIECES + RELAY_LAG))
        def _():
            relay(k - RELAY_LAG)

        @pl.when(k == PIECES + RELAY_LAG - 1)
        def _():
            for t in (3, 2, 1):
                l_copy(t).start()
                q_copy(t).start()

        @pl.when(k >= LAG)
        def _():
            project(k - LAG)

        return carry

    lax.fori_loop(0, PIECES + LAG, step_of, 0)

    for j in range(4):
        s_copy(j).start()
    for j in range(4):
        s_copy(j).wait_recv()
        total = sums[side, j] + partner_sums[j]
        key_rows = jnp.concatenate([total[:, :64], total[:, 128:192]], axis=1)
        value_rows = jnp.concatenate([total[:, 64:128], total[:, 192:]], axis=1)
        frame = frame_at(z1, j, x)
        keys_all[frame, 0:HD] = key_rows.T.astype(jnp.bfloat16)
        values_all[frame] = value_rows.astype(jnp.bfloat16)
        kv_copy(*key_part, 1, j).start()
        kv_copy(*key_part, 0, j).start()
    for j in range(4):
        kv_copy(*value_part, 1, j).start()
    for j in range(4):
        kv_arrival(*key_part, 1, j).wait_recv()
        kv_copy(*key_part, 2, j).start()
    for j in range(4):
        kv_copy(*value_part, 0, j).start()
    for j in range(4):
        kv_arrival(*value_part, 1, j).wait_recv()
        kv_copy(*value_part, 2, j).start()
    own_q.wait()
    for j in range(4):
        kv_arrival(*key_part, 0, j).wait_recv()
        kv_arrival(*key_part, 2, j).wait_recv()

    frames = keys_all.shape[0]
    keys = frames * HD
    gate = jnp.tanh(jnp.full((1, HD), gate_ref[0], jnp.float32))
    factor = HD ** (-0.5) * 1.4426950408889634
    steps = width // (STACK * HD)

    def hidden_of(t):
        last_rows = jnp.broadcast_to(last_all[peer(t), 0:1, :], (HD, HD)).T
        hidden = jnp.where(last_rows < lanes, -1e30, 0.0).astype(jnp.bfloat16)
        return jnp.concatenate([hidden] * STACK, axis=0)

    def weigh(t, hidden, step, exps_ref, dens_ref):
        start = pl.multiple_of(step * STACK * HD, STACK * HD)
        heads = q_all[peer(t), :, pl.ds(start, STACK * HD)]
        stacked = jnp.concatenate([heads[:, i * HD:(i + 1) * HD] for i in range(STACK)], axis=0)
        key_columns = jnp.concatenate([keys_all[frame] for frame in range(frames)], axis=1)
        scores = jnp.dot(
            jnp.concatenate([stacked, hidden], axis=1),
            key_columns,
            preferred_element_type=jnp.float32,
        )
        row_max = jnp.max(scores, axis=1, keepdims=True)
        exps = jnp.exp2((scores - row_max) * factor)
        dens_ref[step] = jnp.broadcast_to(jnp.sum(exps, axis=1, keepdims=True), (STACK * HD, HD))
        exps_ref[step] = exps.astype(jnp.bfloat16)

    def combine(t, step, exps_ref, dens_ref):
        start = pl.multiple_of(step * STACK * HD, STACK * HD)
        value_rows = values_all[...].reshape(keys, HD)
        numerator = jnp.dot(exps_ref[step], value_rows, preferred_element_type=jnp.float32)
        result = (gate * (numerator / dens_ref[step])).astype(jnp.bfloat16)
        out_parts[t, :, pl.ds(start, STACK * HD)] = jnp.concatenate(
            [result[i * HD:(i + 1) * HD] for i in range(STACK)], axis=1
        )

    def run(weighed, combined):
        hidden = hidden_of(weighed[0]) if weighed else None

        def body(step, carry):
            if combined:
                combine(combined[0], step, *combined[1])
            if weighed:
                weigh(weighed[0], hidden, step, *weighed[1])
            return carry

        lax.fori_loop(0, steps, body, 0)

    def queries_here(t):
        l_arrival(t).wait_recv()
        q_arrival(t).wait_recv()

    own, even, odd = (exps_own, dens_own), (exps_even, dens_even), (exps_odd, dens_odd)
    own_hidden = hidden_of(0)
    for step in range(steps // 2):
        weigh(0, own_hidden, step, *own)
    queries_here(3)
    run((3, even), None)
    for j in range(4):
        kv_arrival(*value_part, 0, j).wait_recv()
        kv_arrival(*value_part, 2, j).wait_recv()
    queries_here(2)
    run((2, odd), (3, even))
    o_copy(3).start()
    queries_here(1)
    run((1, even), (2, odd))
    o_copy(2).start()
    run(None, (1, even))
    o_copy(1).start()
    for step in range(steps // 2, steps):
        weigh(0, own_hidden, step, *own)
    run(None, (0, own))
    out_ref[:, columns_of(member)] = out_parts[0]

    def sent(k, carry):
        for kind in range(3):
            w_copy(kind, k).wait_send()
            c_copy(kind, k).wait_send()
        return carry

    lax.fori_loop(0, PIECES, sent, 0)
    for j in range(4):
        s_copy(j).wait_send()
        for kind in range(3):
            kv_copy(*key_part, kind, j).wait_send()
            kv_copy(*value_part, kind, j).wait_send()
    for t in (1, 2, 3):
        l_copy(t).wait_send()
        q_copy(t).wait_send()
        o_copy(t).wait_send()
        o_arrival(t).wait_recv()


def fused_local(vision, kept_index, w_key, w_value, queries, last_frame, attn_gate):
    patches, features = vision.shape[1:]
    rows, row_width = queries.shape
    width = row_width // 4
    depth = features // PIECES
    steps = width // (STACK * HD)
    vmem = pltpu.VMEM
    dma = pltpu.SemaphoreType.DMA
    exps = vmem((steps, STACK * HD, 16 * HD), jnp.bfloat16)
    dens = vmem((steps, STACK * HD, HD), jnp.float32)
    return pl.pallas_call(
        fused_kernel,
        out_shape=jax.ShapeDtypeStruct(queries.shape, jnp.bfloat16),
        in_specs=[pl.BlockSpec(memory_space=pltpu.HBM)] * 6 + [pl.BlockSpec(memory_space=pltpu.SMEM)],
        out_specs=pl.BlockSpec(memory_space=vmem),
        scratch_shapes=[
            vmem((2, patches, depth), jnp.bfloat16),
            vmem((1, HD), jnp.int32),
            vmem((1, rows), jnp.int32),
            vmem((HD, patches), jnp.bfloat16),
            vmem((PIECES, 4, HD, depth), jnp.bfloat16),
            vmem((PIECES, 2, 2, HD, depth), jnp.bfloat16),
            vmem((2, 4, HD, 2 * HD), jnp.float32),
            vmem((4, HD, 2 * HD), jnp.float32),
            vmem((16, 2 * HD, HD), jnp.bfloat16),
            vmem((16, HD, HD), jnp.bfloat16),
            vmem((4, rows, width), jnp.bfloat16),
            vmem((4, 8, HD), jnp.int32),
            exps, exps, exps, dens, dens, dens,
            vmem((4, rows, width), jnp.bfloat16),
            dma((2,)), dma((3,)), dma((2, PIECES)),
            dma((3, PIECES)), dma((3, PIECES)),
            dma((3, PIECES)), dma((3, PIECES)),
            dma((4,)), dma((4,)), dma((4,)), dma((4,)), dma((4,)), dma((4,)),
            dma((3, 4)), dma((3, 4)), dma((3, 4)), dma((3, 4)),
            dma((4,)), dma((4,)),
        ],
        compiler_params=pltpu.CompilerParams(
            collective_id=0, has_side_effects=True, vmem_limit_bytes=56 * 2**20
        ),
    )(vision, kept_index, w_key.T, w_value.T, queries, last_frame.reshape(1, rows), attn_gate)


def fold_frames(running, query_heads, last_rows, key_piece, value_piece):
    row_max, denominator, numerator = running
    frames_here = key_piece.shape[0]
    scores = jnp.einsum(
        "rkgd,fjkd->rkgfj", query_heads, key_piece, preferred_element_type=jnp.float32
    ) * HD ** (-0.5)
    frame_ids = jnp.arange(frames_here, dtype=jnp.int32)
    visible = frame_ids[None, :] <= last_rows[:, None]
    scores = jnp.where(visible[:, None, None, :, None], scores, jnp.float32(-1e30))
    new_max = jnp.maximum(row_max, jnp.max(scores, axis=(3, 4)))
    exps = jnp.exp(scores - new_max[..., None, None])
    new_denominator = jnp.sum(exps, axis=(3, 4))
    weights = exps.astype(jnp.bfloat16)
    added = jnp.einsum("rkgfj,fjkd->rkgd", weights, value_piece, preferred_element_type=jnp.float32)
    return (new_max, new_denominator, added)


def attend(rows_q, rows_last, groups, key_rows, value_rows, attn_gate):
    total_rows, row_width = rows_q.shape
    local_kv = key_rows.shape[2] // HD
    group_size = row_width // HD // local_kv
    group_rows = total_rows // groups
    query_groups = [rows_q.reshape(group_rows, local_kv, group_size, HD)]
    last_groups = [rows_last]
    initial = tuple(
        (
            (
                jnp.full((group_rows, local_kv, group_size), -1e30, jnp.float32),
                jnp.zeros((group_rows, local_kv, group_size), jnp.float32),
                jnp.zeros((group_rows, local_kv, group_size, HD), jnp.float32),
            )
            for member in range(groups)
        )
    )
    key_piece = lax.all_gather(key_rows, "blk", axis=0, tiled=True)
    value_piece = lax.all_gather(value_rows, "blk", axis=0, tiled=True)
    frames_here = key_piece.shape[0]
    key_piece = key_piece.reshape(frames_here, key_piece.shape[1], local_kv, HD)
    value_piece = value_piece.reshape(frames_here, value_piece.shape[1], local_kv, HD)
    member = 0
    query_heads = query_groups[member]
    last_rows = last_groups[member]
    state_new = fold_frames(initial[member], query_heads, last_rows, key_piece, value_piece)
    updated = [state_new]
    results = tuple(updated)
    gate_factor = jnp.tanh(attn_gate[0])
    pieces_out = [
        (gate_factor * (numerator / denominator[..., None])).reshape(group_rows, row_width)
        for row_max, denominator, numerator in results
    ]
    return pieces_out[0].astype(jnp.bfloat16)


def local(vision, kept_index, w_key, w_value, queries, last_frame, attn_gate):
    chosen = vision[0][kept_index[0]]
    stacked = jnp.stack([w_key, w_value])
    partial_value = jnp.einsum(
        "td,sdc->stc",
        chosen,
        lax.all_gather(stacked, "blk", axis=2, tiled=True),
        preferred_element_type=jnp.float32,
    )
    summed = lax.psum_scatter(partial_value, "head", scatter_dimension=2, tiled=True).astype(
        jnp.bfloat16
    )
    key_rows = summed[0][None]
    value_rows = summed[1][None]
    return attend(queries, last_frame, 1, key_rows, value_rows, attn_gate)


def solution(mesh):
    in_specs = (
        P("blk", None, "head"),
        P("blk", None),
        P("head", "blk"),
        P("head", "blk"),
        P("blk", "head"),
        P("blk"),
        P(),
    )
    out_specs = P("blk", "head")
    if dict(mesh.shape) == {"blk": 16, "head": 2}:
        return jax.shard_map(
            fused_local, mesh=mesh, in_specs=in_specs, out_specs=out_specs, check_vma=False
        )
    return jax.shard_map(local, mesh=mesh, in_specs=in_specs, out_specs=out_specs, check_vma=False)
```

```python
import jax
import jax.numpy as jnp
from jax import lax
from jax.experimental import pallas as pl
from jax.experimental.pallas import tpu as pltpu
from jax.sharding import PartitionSpec as P

HD = 128
MESH = pl.DeviceIdType.MESH
PIECES = 16
RELAY_LAG = 2
LAG = 4
STACK = 4


def fused_kernel(
    vision_ref, index_hbm, w_key_ref, w_value_ref, q_ref, last_hbm, gate_ref, out_ref,
    vision_buf, index_ref, last_ref, onehot, chosen, weights, sums, partner_sums, keys_all,
    values_all, q_all, last_all, exps_own, exps_even, exps_odd, dens_own, dens_even, dens_odd,
    out_parts, vision_sem, small_sem, load_sem,
    w_send, w_recv, c_send, c_recv, q_send, q_recv, l_send, l_recv,
    s_send, s_recv, k_send, k_recv, v_send, v_recv, o_send, o_recv,
):
    blk = lax.axis_index("blk")
    side = lax.axis_index("head")
    z1, member, x = blk // 8, (blk % 8) // 2, blk % 2
    z0, y = member // 2, member % 2
    frame_at = lambda zz, mm, xx: zz * 8 + mm * 2 + xx
    to_x = (frame_at(z1, member, 1 - x), side)
    to_z1 = (frame_at(1 - z1, member, x), side)
    to_y = (frame_at(z1, z0 * 2 + 1 - y, x), side)
    to_z0 = (frame_at(z1, (1 - z0) * 2 + y, x), side)
    to_diagonal = (frame_at(z1, (1 - z0) * 2 + 1 - y, x), side)
    to_core = (blk, 1 - side)
    partners = (to_x, to_z1, to_y, to_z0, to_diagonal, to_core)

    def send(src, dst, send_sem, recv_sem, device):
        return pltpu.make_async_remote_copy(
            src_ref=src, dst_ref=dst, send_sem=send_sem, recv_sem=recv_sem,
            device_id=device, device_id_type=MESH,
        )

    depth = chosen.shape[3]
    patches = vision_buf.shape[1]

    def vision_copy(k):
        columns = pl.ds(pl.multiple_of(k * depth, depth), depth)
        slot = lax.rem(k, 2)
        return pltpu.make_async_copy(
            vision_ref.at[0, :, columns], vision_buf.at[slot], vision_sem.at[slot]
        )

    def w_copy(kind, k):
        slot = weights.at[k, z1 if kind < 2 else 1 - z1, x]
        return send(slot, slot, w_send.at[kind, k], w_recv.at[kind, k], to_z1 if kind == 1 else to_x)

    def w_arrival(kind, k):
        slot = weights.at[k, z1 if kind == 0 else 1 - z1, x if kind == 1 else 1 - x]
        return send(slot, slot, w_send.at[kind, k], w_recv.at[kind, k], to_x)

    def c_copy(kind, k):
        slot = chosen.at[k, member if kind < 2 else (1 - z0) * 2 + y]
        return send(slot, slot, c_send.at[kind, k], c_recv.at[kind, k], to_z0 if kind == 1 else to_y)

    def c_arrival(kind, k):
        from_z0 = z0 if kind == 0 else 1 - z0
        from_y = y if kind == 1 else 1 - y
        slot = chosen.at[k, from_z0 * 2 + from_y]
        return send(slot, slot, c_send.at[kind, k], c_recv.at[kind, k], to_y)

    def kv_copy(held, send_sem, recv_sem, kind, j):
        slot = held.at[frame_at(z1 if kind < 2 else 1 - z1, j, x), pl.ds(0, HD)]
        return send(slot, slot, send_sem.at[kind, j], recv_sem.at[kind, j], to_z1 if kind == 1 else to_x)

    def kv_arrival(held, send_sem, recv_sem, kind, j):
        frame = frame_at(z1 if kind == 0 else 1 - z1, j, x if kind == 1 else 1 - x)
        slot = held.at[frame, pl.ds(0, HD)]
        return send(slot, slot, send_sem.at[kind, j], recv_sem.at[kind, j], to_x)

    key_part = (keys_all, k_send, k_recv)
    value_part = (values_all, v_send, v_recv)

    width = q_all.shape[2]

    def peer(t):
        return (1 - z0 if t // 2 else z0) * 2 + (1 - y if t % 2 else y)

    def columns_of(m):
        return pl.ds(pl.multiple_of(m * width, width), width)

    def q_copy(t):
        target = (frame_at(z1, peer(t), x), side)
        return send(q_ref.at[:, columns_of(peer(t))], q_all.at[member], q_send.at[t], q_recv.at[t], target)

    def q_arrival(t):
        slot = q_all.at[peer(t)]
        return send(slot, slot, q_send.at[t], q_recv.at[t], to_y)

    def l_copy(t):
        target = (frame_at(z1, peer(t), x), side)
        return send(last_all.at[member], last_all.at[member], l_send.at[t], l_recv.at[t], target)

    def l_arrival(t):
        slot = last_all.at[peer(t)]
        return send(slot, slot, l_send.at[t], l_recv.at[t], to_y)

    def o_copy(t):
        target = (frame_at(z1, peer(t), x), side)
        return send(out_parts.at[t], out_ref.at[:, columns_of(member)], o_send.at[t], o_recv.at[t], target)

    def o_arrival(t):
        slot = out_ref.at[:, columns_of(peer(t))]
        return send(slot, slot, o_send.at[t], o_recv.at[t], to_y)

    def s_copy(j):
        return send(sums.at[1 - side, j], partner_sums.at[j], s_send.at[j], s_recv.at[j], to_core)

    def w_load(which, k):
        columns = pl.ds(pl.multiple_of(k * depth, depth), depth)
        return pltpu.make_async_copy(
            (w_key_ref, w_value_ref)[which].at[:, columns],
            weights.at[k, z1, x, pl.ds(which * 64, 64)], load_sem.at[which, k],
        )

    own_q = pltpu.make_async_copy(q_ref.at[:, columns_of(member)], q_all.at[member], small_sem.at[0])
    index_copy = pltpu.make_async_copy(index_hbm, index_ref, small_sem.at[1])
    last_copy = pltpu.make_async_copy(last_hbm, last_ref, small_sem.at[2])

    barrier = pltpu.get_barrier_semaphore()
    for device in partners:
        pl.semaphore_signal(barrier, inc=1, device_id=device, device_id_type=MESH)

    def load_weights(k, carry):
        w_load(0, k).start()
        w_load(1, k).start()
        return carry

    index_copy.start()
    last_copy.start()
    lax.fori_loop(0, PIECES, load_weights, 0)
    vision_copy(0).start()
    vision_copy(1).start()
    own_q.start()
    pl.semaphore_wait(barrier, len(partners))

    def send_weights(k):
        w_load(0, k).wait()
        w_load(1, k).wait()
        w_copy(1, k).start()
        w_copy(0, k).start()

    send_weights(0)
    send_weights(1)
    index_copy.wait()
    last_copy.wait()
    index_rows = jnp.broadcast_to(index_ref[...], (HD, HD)).T
    lanes = lax.broadcasted_iota(jnp.int32, (HD, HD), 1)
    for start in range(0, patches, HD):
        stop = min(start + HD, patches)
        onehot[:, start:stop] = jnp.where(index_rows == lanes + start, 1.0, 0.0).astype(
            jnp.bfloat16
        )[:, :stop - start]

    def choose(k):
        vision_copy(k).wait()
        picked = jnp.dot(
            onehot[...], vision_buf[lax.rem(k, 2)], preferred_element_type=jnp.float32
        )
        chosen[k, member] = picked.astype(jnp.bfloat16)
        c_copy(1, k).start()
        c_copy(0, k).start()

    last_all[member] = jnp.broadcast_to(last_ref[...], (8, HD))
    sums[...] = jnp.zeros_like(sums)
    feature = lax.broadcasted_iota(jnp.int32, (HD, HD), 0)
    for frame in range(keys_all.shape[0]):
        keys_all[frame, HD:] = jnp.where(feature == frame, 1.0, 0.0).astype(jnp.bfloat16)

    def project(k):
        for kind in (0, 2):
            w_arrival(kind, k).wait_recv()
            c_arrival(kind, k).wait_recv()
        rows = chosen[k].reshape(4 * HD, depth)
        for group in range(2):
            columns = weights[k, group].reshape(2 * HD, depth)
            added = lax.dot_general(
                rows, columns, (((1,), (1,)), ((), ())), preferred_element_type=jnp.float32
            )
            sums[group] += added.reshape(4, HD, 2 * HD)

    def relay(k):
        w_arrival(1, k).wait_recv()
        w_copy(2, k).start()
        c_arrival(1, k).wait_recv()
        c_copy(2, k).start()

    def step_of(k, carry):
        @pl.when(k < PIECES)
        def _():
            choose(k)

        @pl.when(k + 2 < PIECES)
        def _():
            vision_copy(k + 2).start()
            send_weights(k + 2)

        @pl.when((k >= RELAY_LAG) & (k < PIECES + RELAY_LAG))
        def _():
            relay(k - RELAY_LAG)

        @pl.when(k == PIECES + RELAY_LAG - 1)
        def _():
            for t in (3, 2, 1):
                l_copy(t).start()
                q_copy(t).start()

        @pl.when(k >= LAG)
        def _():
            project(k - LAG)

        return carry

    lax.fori_loop(0, PIECES + LAG, step_of, 0)

    for j in range(4):
        s_copy(j).start()
    for j in range(4):
        s_copy(j).wait_recv()
        total = sums[side, j] + partner_sums[j]
        key_rows = jnp.concatenate([total[:, :64], total[:, 128:192]], axis=1)
        value_rows = jnp.concatenate([total[:, 64:128], total[:, 192:]], axis=1)
        frame = frame_at(z1, j, x)
        keys_all[frame, 0:HD] = key_rows.T.astype(jnp.bfloat16)
        values_all[frame] = value_rows.astype(jnp.bfloat16)
        kv_copy(*key_part, 1, j).start()
        kv_copy(*key_part, 0, j).start()
    for j in range(4):
        kv_copy(*value_part, 1, j).start()
    for j in range(4):
        kv_arrival(*key_part, 1, j).wait_recv()
        kv_copy(*key_part, 2, j).start()
    for j in range(4):
        kv_copy(*value_part, 0, j).start()
    for j in range(4):
        kv_arrival(*value_part, 1, j).wait_recv()
        kv_copy(*value_part, 2, j).start()
    own_q.wait()
    for j in range(4):
        kv_arrival(*key_part, 0, j).wait_recv()
        kv_arrival(*key_part, 2, j).wait_recv()

    frames = keys_all.shape[0]
    keys = frames * HD
    gate = jnp.tanh(jnp.full((1, HD), gate_ref[0], jnp.float32))
    factor = HD ** (-0.5) * 1.4426950408889634
    steps = width // (STACK * HD)

    def hidden_of(t):
        last_rows = jnp.broadcast_to(last_all[peer(t), 0:1, :], (HD, HD)).T
        hidden = jnp.where(last_rows < lanes, -1e30, 0.0).astype(jnp.bfloat16)
        return jnp.concatenate([hidden] * STACK, axis=0)

    def weigh(t, hidden, step, exps_ref, dens_ref):
        start = pl.multiple_of(step * STACK * HD, STACK * HD)
        heads = q_all[peer(t), :, pl.ds(start, STACK * HD)]
        stacked = jnp.concatenate([heads[:, i * HD:(i + 1) * HD] for i in range(STACK)], axis=0)
        key_columns = jnp.concatenate([keys_all[frame] for frame in range(frames)], axis=1)
        scores = jnp.dot(
            jnp.concatenate([stacked, hidden], axis=1),
            key_columns,
            preferred_element_type=jnp.float32,
        )
        row_max = jnp.max(scores, axis=1, keepdims=True)
        exps = jnp.exp2((scores - row_max) * factor)
        dens_ref[step] = jnp.broadcast_to(jnp.sum(exps, axis=1, keepdims=True), (STACK * HD, HD))
        exps_ref[step] = exps.astype(jnp.bfloat16)

    def combine(t, step, exps_ref, dens_ref):
        start = pl.multiple_of(step * STACK * HD, STACK * HD)
        value_rows = values_all[...].reshape(keys, HD)
        numerator = jnp.dot(exps_ref[step], value_rows, preferred_element_type=jnp.float32)
        result = (gate * (numerator / dens_ref[step])).astype(jnp.bfloat16)
        out_parts[t, :, pl.ds(start, STACK * HD)] = jnp.concatenate(
            [result[i * HD:(i + 1) * HD] for i in range(STACK)], axis=1
        )

    def run(weighed, combined):
        hidden = hidden_of(weighed[0]) if weighed else None

        def body(step, carry):
            if combined:
                combine(combined[0], step, *combined[1])
            if weighed:
                weigh(weighed[0], hidden, step, *weighed[1])
            return carry

        lax.fori_loop(0, steps, body, 0)

    def queries_here(t):
        l_arrival(t).wait_recv()
        q_arrival(t).wait_recv()

    own, even, odd = (exps_own, dens_own), (exps_even, dens_even), (exps_odd, dens_odd)
    own_hidden = hidden_of(0)
    for step in range(steps // 2):
        weigh(0, own_hidden, step, *own)
    queries_here(3)
    run((3, even), None)
    for j in range(4):
        kv_arrival(*value_part, 0, j).wait_recv()
        kv_arrival(*value_part, 2, j).wait_recv()
    queries_here(2)
    run((2, odd), (3, even))
    o_copy(3).start()
    queries_here(1)
    run((1, even), (2, odd))
    o_copy(2).start()
    run(None, (1, even))
    o_copy(1).start()
    for step in range(steps // 2, steps):
        weigh(0, own_hidden, step, *own)
    run(None, (0, own))
    out_ref[:, columns_of(member)] = out_parts[0]

    def sent(k, carry):
        for kind in range(3):
            w_copy(kind, k).wait_send()
            c_copy(kind, k).wait_send()
        return carry

    lax.fori_loop(0, PIECES, sent, 0)
    for j in range(4):
        s_copy(j).wait_send()
        for kind in range(3):
            kv_copy(*key_part, kind, j).wait_send()
            kv_copy(*value_part, kind, j).wait_send()
    for t in (1, 2, 3):
        l_copy(t).wait_send()
        q_copy(t).wait_send()
        o_copy(t).wait_send()
        o_arrival(t).wait_recv()


def fused_local(vision, kept_index, w_key, w_value, queries, last_frame, attn_gate):
    patches, features = vision.shape[1:]
    rows, row_width = queries.shape
    width = row_width // 4
    depth = features // PIECES
    steps = width // (STACK * HD)
    vmem = pltpu.VMEM
    dma = pltpu.SemaphoreType.DMA
    exps = vmem((steps, STACK * HD, 16 * HD), jnp.bfloat16)
    dens = vmem((steps, STACK * HD, HD), jnp.float32)
    return pl.pallas_call(
        fused_kernel,
        out_shape=jax.ShapeDtypeStruct(queries.shape, jnp.bfloat16),
        in_specs=[pl.BlockSpec(memory_space=pltpu.HBM)] * 6 + [pl.BlockSpec(memory_space=pltpu.SMEM)],
        out_specs=pl.BlockSpec(memory_space=vmem),
        scratch_shapes=[
            vmem((2, patches, depth), jnp.bfloat16),
            vmem((1, HD), jnp.int32),
            vmem((1, rows), jnp.int32),
            vmem((HD, patches), jnp.bfloat16),
            vmem((PIECES, 4, HD, depth), jnp.bfloat16),
            vmem((PIECES, 2, 2, HD, depth), jnp.bfloat16),
            vmem((2, 4, HD, 2 * HD), jnp.float32),
            vmem((4, HD, 2 * HD), jnp.float32),
            vmem((16, 2 * HD, HD), jnp.bfloat16),
            vmem((16, HD, HD), jnp.bfloat16),
            vmem((4, rows, width), jnp.bfloat16),
            vmem((4, 8, HD), jnp.int32),
            exps, exps, exps, dens, dens, dens,
            vmem((4, rows, width), jnp.bfloat16),
            dma((2,)), dma((3,)), dma((2, PIECES)),
            dma((3, PIECES)), dma((3, PIECES)),
            dma((3, PIECES)), dma((3, PIECES)),
            dma((4,)), dma((4,)), dma((4,)), dma((4,)), dma((4,)), dma((4,)),
            dma((3, 4)), dma((3, 4)), dma((3, 4)), dma((3, 4)),
            dma((4,)), dma((4,)),
        ],
        compiler_params=pltpu.CompilerParams(
            collective_id=0, has_side_effects=True, vmem_limit_bytes=56 * 2**20
        ),
    )(vision, kept_index, w_key.T, w_value.T, queries, last_frame.reshape(1, rows), attn_gate)


def fold_frames(running, query_heads, last_rows, key_piece, value_piece):
    row_max, denominator, numerator = running
    frames_here = key_piece.shape[0]
    scores = jnp.einsum(
        "rkgd,fjkd->rkgfj", query_heads, key_piece, preferred_element_type=jnp.float32
    ) * HD ** (-0.5)
    frame_ids = jnp.arange(frames_here, dtype=jnp.int32)
    visible = frame_ids[None, :] <= last_rows[:, None]
    scores = jnp.where(visible[:, None, None, :, None], scores, jnp.float32(-1e30))
    new_max = jnp.maximum(row_max, jnp.max(scores, axis=(3, 4)))
    exps = jnp.exp(scores - new_max[..., None, None])
    new_denominator = jnp.sum(exps, axis=(3, 4))
    weights = exps.astype(jnp.bfloat16)
    added = jnp.einsum("rkgfj,fjkd->rkgd", weights, value_piece, preferred_element_type=jnp.float32)
    return (new_max, new_denominator, added)


def attend(rows_q, rows_last, groups, key_rows, value_rows, attn_gate):
    total_rows, row_width = rows_q.shape
    local_kv = key_rows.shape[2] // HD
    group_size = row_width // HD // local_kv
    group_rows = total_rows // groups
    query_groups = [rows_q.reshape(group_rows, local_kv, group_size, HD)]
    last_groups = [rows_last]
    initial = tuple(
        (
            (
                jnp.full((group_rows, local_kv, group_size), -1e30, jnp.float32),
                jnp.zeros((group_rows, local_kv, group_size), jnp.float32),
                jnp.zeros((group_rows, local_kv, group_size, HD), jnp.float32),
            )
            for member in range(groups)
        )
    )
    key_piece = lax.all_gather(key_rows, "blk", axis=0, tiled=True)
    value_piece = lax.all_gather(value_rows, "blk", axis=0, tiled=True)
    frames_here = key_piece.shape[0]
    key_piece = key_piece.reshape(frames_here, key_piece.shape[1], local_kv, HD)
    value_piece = value_piece.reshape(frames_here, value_piece.shape[1], local_kv, HD)
    member = 0
    query_heads = query_groups[member]
    last_rows = last_groups[member]
    state_new = fold_frames(initial[member], query_heads, last_rows, key_piece, value_piece)
    updated = [state_new]
    results = tuple(updated)
    gate_factor = jnp.tanh(attn_gate[0])
    pieces_out = [
        (gate_factor * (numerator / denominator[..., None])).reshape(group_rows, row_width)
        for row_max, denominator, numerator in results
    ]
    return pieces_out[0].astype(jnp.bfloat16)


def local(vision, kept_index, w_key, w_value, queries, last_frame, attn_gate):
    chosen = vision[0][kept_index[0]]
    stacked = jnp.stack([w_key, w_value])
    partial_value = jnp.einsum(
        "td,sdc->stc",
        chosen,
        lax.all_gather(stacked, "blk", axis=2, tiled=True),
        preferred_element_type=jnp.float32,
    )
    summed = lax.psum_scatter(partial_value, "head", scatter_dimension=2, tiled=True).astype(
        jnp.bfloat16
    )
    key_rows = summed[0][None]
    value_rows = summed[1][None]
    return attend(queries, last_frame, 1, key_rows, value_rows, attn_gate)


def solution(mesh):
    in_specs = (
        P("blk", None, "head"),
        P("blk", None),
        P("head", "blk"),
        P("head", "blk"),
        P("blk", "head"),
        P("blk"),
        P(),
    )
    out_specs = P("blk", "head")
    if dict(mesh.shape) == {"blk": 16, "head": 2}:
        return jax.shard_map(
            fused_local, mesh=mesh, in_specs=in_specs, out_specs=out_specs, check_vma=False
        )
    return jax.shard_map(local, mesh=mesh, in_specs=in_specs, out_specs=out_specs, check_vma=False)
```
